256 devices in a mesh: tm: 32 (over z, x), rows: 8 (over y, core).
Axes of the slice: x: 4, y: 4, z: 8, core: 2. Of those that a mesh axis runs over, the one named last changes fastest.
Arguments:
- clip: float32 [128, 16, 32, 128], P('tm', 'rows'), may hold values from -6 to 6
- kernel_one: float32 [3, 3, 3, 128, 128], replicated, may hold values from -0.109375 to 0.109375
- kernel_two: float32 [3, 3, 3, 128, 128], replicated, may hold values from -0.109375 to 0.109375
- cotangent: float32 [128, 16, 32, 128], P('tm', 'rows'), may hold values from -6 to 6
Outputs:
- block_out: float32 [128, 16, 32, 128], P('tm', 'rows')
- grad_clip: float32 [128, 16, 32, 128], P('tm', 'rows')
- grad_one: float32 [3, 3, 3, 128, 128], replicated
- grad_two: float32 [3, 3, 3, 128, 128], replicated
The draws below stay inside these ranges and needn't reach their ends.
All inputs are finite; a program needn't handle non-finite values.
Results may differ from the reference program's by a relative error of at most 0.00014.
Values sent between devices are 32-bit elements; how exact they have to be, the bound alone decides.
A program may use at most 128 MiB of HBM per device.

```python
import math
import jax
import jax.numpy as jnp
from jax import lax

CH = 128
WIDTH = 32
FRAMES = 128
HEIGHT = 16


def block_levels(own_key, dims, shards, smallest, largest):
    loudness, own = 1.0, jax.random.fold_in(own_key, 6)
    for dim, blocks in shards:
        draws = jnp.exp(jax.random.uniform(jax.random.fold_in(own, dim), (blocks,), jnp.float32, smallest / len(shards), largest / len(shards)))
        loudness = loudness * jnp.repeat(draws, dims[dim] // blocks).reshape([-1 if axis == dim else 1 for axis in range(len(dims))])
    return loudness


def scatter_about(rng, dims, spread, limit, cuts=(), held_as=jnp.bfloat16):
    loudness = block_levels(rng, dims, cuts, -0.22, 0.18) if cuts else 1.0
    values = jax.random.normal(rng, dims, jnp.float32) * spread * loudness
    return jnp.minimum(jnp.maximum(values, -limit), limit).astype(held_as)


def setup_inputs(seed: int = 0) -> dict:
    streams_of = jax.random.split(jax.random.key(seed), 5)
    clip = scatter_about(streams_of[0], (FRAMES, HEIGHT, WIDTH, CH), 1.0, 6.0, ((0, 32), (1, 8)), jnp.float32)
    kernel_one = scatter_about(streams_of[1], (3, 3, 3, CH, CH), (27 * CH) ** -0.5, 0.109375, (), jnp.float32)
    kernel_two = scatter_about(streams_of[2], (3, 3, 3, CH, CH), (27 * CH) ** -0.5, 0.109375, (), jnp.float32)
    cotangent = scatter_about(streams_of[3], (FRAMES, HEIGHT, WIDTH, CH), 1.0, 6.0, ((0, 32), (1, 8)), jnp.float32)
    return {"clip": clip, "kernel_one": kernel_one, "kernel_two": kernel_two, "cotangent": cotangent}


def convolve(field, kernel):
    result = lax.conv_general_dilated(field[None], kernel, (1, 1, 1), ((2, 0), (1, 1), (1, 1)), dimension_numbers=('NDHWC', 'DHWIO', 'NDHWC'), precision=lax.Precision.HIGHEST)
    return result[0]

def forward(clip, kernel_one, kernel_two):
    return clip + convolve(jax.nn.silu(convolve(clip, kernel_one)), kernel_two)

def reference(clip, kernel_one, kernel_two, cotangent):
    block_out, pullback = jax.vjp(forward, clip, kernel_one, kernel_two)
    grad_clip, grad_one, grad_two = pullback(cotangent)
    factor = 1.0 / math.sqrt(FRAMES * HEIGHT * WIDTH)
    return (block_out, grad_clip, grad_one * factor, grad_two * factor)
```

```python
import jax
import jax.numpy as jnp
from jax import lax
from jax.experimental import pallas as pl
from jax.experimental.pallas import tpu as pltpu
from jax.sharding import PartitionSpec as P

MESH = pl.DeviceIdType.MESH
F32 = jnp.float32
BF16 = jnp.bfloat16
TAPS = [(a, b, c) for a in range(3) for b in range(3) for c in range(3)]
GROUPS = [TAPS[0:8], TAPS[8:16], TAPS[16:24], TAPS[24:27]]
STREAMS = [(0, 7, True, 27), (7, 7, False, 28), (14, 7, True, 29), (21, 6, False, 30)]
COPIES = 200
Q = 1.0 / 256.0


def tap_index(tap):
    return (tap[0] * 3 + tap[1]) * 3 + tap[2]


def split(v):
    hi = v.astype(BF16)
    return hi, (v - hi.astype(F32)).astype(BF16)


def kernel(
    clip_ref, cot_ref, k1_ref, k2_ref,
    block_ref, gclip_ref, sums,
    kf, kh, kl, ext, ext2, cols, acc, pre, fixed, part, r1, r2, r3, r4, rz,
    send_sem, recv_sem, load_sem,
):
    tm = lax.axis_index("tm")
    rows = lax.axis_index("rows")
    x, z = lax.rem(tm, 4), lax.div(tm, 4)
    core, y = lax.rem(rows, 2), lax.div(rows, 2)

    def at(xx, yy, zz):
        return (lax.rem(zz + 8, 8) * 4 + lax.rem(xx + 4, 4), lax.rem(yy + 4, 4) * 2 + core)

    partner_row = y * 2 + 1 - core
    outer_row = lax.rem(rows + 2 * core - 1 + 8, 8)
    tm_next, tm_prev = lax.rem(tm + 1, 32), lax.rem(tm + 31, 32)
    partner = (tm, partner_row)

    loads = []
    for n, k_ref in enumerate((k1_ref, k2_ref)):
        loads.append(pltpu.make_async_copy(k_ref, kf.at[n], load_sem.at[n]))
        loads[-1].start()

    peers = [partner, (tm, outer_row)]
    for t in (tm_next, tm_prev):
        peers += [(t, rows), (t, partner_row), (t, outer_row)]
    peers += [at(x + 1, y, z), at(x - 1, y, z), at(x, y + 1, z), at(x, y - 1, z)]
    peers += [at(x, y, z + d) for d in range(1, 8)]
    barrier = pltpu.get_barrier_semaphore()
    for peer in peers:
        pl.semaphore_signal(barrier, inc=1, device_id=peer, device_id_type=MESH)

    own = pl.ds(1 + 2 * core, 2)
    ext[0, 2:6, own] = clip_ref[...]
    ext[1, 0:4, own] = cot_ref[...]
    part[27:32] = jnp.zeros((5, 16, 8, 128), F32)
    pl.semaphore_wait(barrier, len(peers))

    started = []

    def put(src, dst, device):
        n = len(started)
        copy = pltpu.make_async_remote_copy(
            src_ref=src, dst_ref=dst, send_sem=send_sem.at[n], recv_sem=recv_sem.at[n],
            device_id=device, device_id_type=MESH,
        )
        copy.start()
        started.append(copy)
        return copy

    edge, edge_there, inner = 1 + 3 * core, 5 - 5 * core, 2 + core
    sides = ((0, pl.ds(2, 4), pl.ds(4, 2), pl.ds(0, 2), tm_next), (1, pl.ds(0, 4), pl.ds(0, 2), pl.ds(4, 2), tm_prev))

    def to_partner(field):
        return [put(field.at[n, mine, own], field.at[n, mine, own], partner) for n, mine, _, _, _ in sides]

    def to_others(field, across):
        out = []
        for n, mine, src, dst, there in sides:
            out.append(put(field.at[n, src, own], field.at[n, dst, own], (there, rows)))
            out.append(put(field.at[n, mine, edge], field.at[n, mine, edge_there], (tm, outer_row)))
            out.append(put(field.at[n, src, across], field.at[n, dst, across], (there, partner_row)))
            out.append(put(field.at[n, src, edge], field.at[n, dst, edge_there], (there, outer_row)))
        return out

    halo = to_others(ext, own) + to_partner(ext)

    for load in loads:
        load.wait()

    def split_tap(t, _):
        for n in range(2):
            kh[n, t], kl[n, t] = split(kf[n, t])
        return 0

    lax.fori_loop(0, 27, split_tap, 0)
    for copy in halo:
        copy.wait_recv()
    far_row = put(ext.at[core, :, 5 * core], ext.at[core, :, 5 * core], partner)

    at_column = lax.broadcasted_iota(jnp.int32, (32, 128), 0)

    def columns(field, n, row):
        inside = jnp.logical_not(((row == 0) & (y == 0)) | ((row == 5) & (y == 3)))
        for f in range(6):
            keep = inside
            if n == 0 and f < 2:
                keep = keep & (tm > 0)
            if n == 1 and f > 3:
                keep = keep & (tm < 31)
            v = jnp.where(keep, field[n, f, row], 0.0)
            hi = v.astype(BF16).astype(F32)
            lo = v - hi
            for h, piece in enumerate((hi, lo)):
                cols[n, h, 0, f, row] = jnp.where(at_column == 0, 0.0, pltpu.roll(piece, 1, 0)).astype(BF16)
                cols[n, h, 1, f, row] = piece.astype(BF16)
                cols[n, h, 2, f, row] = jnp.where(at_column == 31, 0.0, pltpu.roll(piece, 31, 0)).astype(BF16)

    def convolve(n, kernel_at, turned):
        for g, group in enumerate(GROUPS):
            left, right = [], []
            for a, b, c in group:
                at_tap = tap_index((a, b, c))
                i, j, k = (2 - a, 2 - b, 2 - c) if turned else (a, b, c)
                window = [cols[n, h, k, i : i + 4, pl.ds(2 * core + j, 2)].reshape(256, 128) for h in range(2)]
                left.append(jnp.concatenate(window, 0))
                right.append(jnp.concatenate([kh[kernel_at, at_tap], kl[kernel_at, at_tap]], 0 if turned else 1))
            left = jnp.concatenate(left, 1)
            right = jnp.concatenate(right, 1 if turned else 0)
            product = lax.dot_general(left, right, (((1,), (1 if turned else 0,)), ((), ())), preferred_element_type=F32)
            if g == 0:
                acc[...] = product
            else:
                acc[...] += product
        total = acc[0:256, 0:128] + (acc[0:256, 128:256] + acc[256:512, 0:128]) + acc[256:512, 128:256]
        return total.reshape(4, 2, 32, 128)

    def near_columns(field, n):
        def one(j, _):
            columns(field, n, 2 * core + j)
            return 0

        lax.fori_loop(0, 4, one, 0)

    near_columns(ext, 0)
    pre[...] = convolve(0, 0, False)
    near_columns(ext, 1)
    d_active = convolve(1, 1, True)
    v = pre[...]
    s = jax.nn.sigmoid(v)
    ext2[0, 2:6, own] = v * s
    ext2[1, 0:4, own] = d_active * s * (1.0 + v * (1.0 - s))
    swap = to_partner(ext2)

    far_row.wait_recv()

    @pl.when(core == 0)
    def _():
        for row in (4, 5):
            columns(ext, 1, row)

    @pl.when(core == 1)
    def _():
        for row in (0, 1):
            columns(ext, 0, row)

    for copy in swap:
        copy.wait_recv()
    whole = ext2[core, pl.ds(2 - 2 * core, 4), 1:5].reshape(512, 128)
    fixed[0:128], fixed[128:256] = split(whole.T)
    halo2 = []

    def gradient(tap):
        a, b, c = (core * t + (1 - core) * (2 - t) for t in tap)
        right = [cols[1 - core, h, c, pl.ds(a, 4), pl.ds(b, 4)].reshape(512, 128) for h in range(2)]
        m = jnp.dot(fixed[...], jnp.concatenate(right, 1), preferred_element_type=F32)
        m = m[0:128, 0:128] + (m[0:128, 128:256] + m[128:256, 0:128]) + m[128:256, 128:256]
        part[tap_index(tap)] = jnp.where(core == 1, m.T, m).reshape(16, 8, 128)

    def stream(first, count, x_first, pad):
        taps = pl.ds(first, count)
        half = count // 2
        taps_a, taps_b = pl.ds(first, half), pl.ds(first + half, count - half)
        along_x, along_y = (at(x + 1, y, z), at(x - 1, y, z)), (at(x, y + 1, z), at(x, y - 1, z))
        p, s = (x, y) if x_first else (y, x)
        (plus, minus), (plus2, minus2) = (along_x, along_y) if x_first else (along_y, along_x)
        p_next, p_prev, p_far = lax.rem(p + 1, 4), lax.rem(p + 3, 4), lax.rem(p + 2, 4)
        t_next, t_prev, t_far = (4 * p + lax.rem(s + d, 4) for d in (1, 3, 2))
        t_own = 4 * p + s
        mine = sums.at[core]

        def slot(zz):
            return first + zz + lax.div(zz, count) * (pad - first - count)

        for tap in TAPS[first : first + count]:
            gradient(tap)
        a = put(part.at[taps, pl.ds(4 * p_far, 2)], r1.at[0, taps], plus)
        b = put(part.at[taps, pl.ds(4 * p_far + 2, 2)], r1.at[1, taps], minus)
        yield
        a.wait_recv()
        part[taps, pl.ds(4 * p_next, 2)] += r1[0, taps]
        a = put(part.at[taps, pl.ds(4 * p_next, 4)], r2.at[0, taps], plus)
        b.wait_recv()
        part[taps, pl.ds(4 * p_prev + 2, 2)] += r1[1, taps]
        b = put(part.at[taps, pl.ds(4 * p_prev, 4)], r2.at[1, taps], minus)
        yield
        a.wait_recv()
        b.wait_recv()
        part[taps, pl.ds(4 * p, 4)] += r2[0, taps] + r2[1, taps]
        a = put(part.at[taps_a, t_far], r3.at[0, taps_a], plus2)
        b = put(part.at[taps_b, t_far], r3.at[1, taps_b], minus2)
        yield
        a.wait_recv()
        part[taps_a, t_next] += r3[0, taps_a]
        a = put(part.at[taps, t_next], r4.at[0, taps], plus2)
        b.wait_recv()
        part[taps_b, t_prev] += r3[1, taps_b]
        b = put(part.at[taps, t_prev], r4.at[1, taps], minus2)
        yield
        a.wait_recv()
        b.wait_recv()
        part[taps, t_own] += r4[0, taps] + r4[1, taps]
        along_z = []
        which = pad - 27
        for d in range(1, 8):
            there = lax.rem(z + d, 8)
            along_z.append(put(part.at[slot(there), t_own], rz.at[which, z], at(x, y, there)))
        yield
        total = part[slot(z), t_own]
        for d in range(1, 8):
            along_z[d - 1].wait_recv()
            total = total + rz[which, lax.rem(z - d + 8, 8)]
        mine[slot(z), t_own] = total * Q
        along_z = []
        for d in range(1, 8):
            along_z.append(put(mine.at[slot(z), t_own], mine.at[slot(z), t_own], at(x, y, lax.rem(z + d, 8))))
        yield
        for copy in along_z:
            copy.wait_recv()
        a = put(mine.at[taps, t_own], mine.at[taps, t_own], plus2)
        b = put(mine.at[taps, t_own], mine.at[taps, t_own], minus2)
        yield
        a.wait_recv()
        a = put(mine.at[taps_a, t_prev], mine.at[taps_a, t_prev], plus2)
        b.wait_recv()
        b = put(mine.at[taps_b, t_next], mine.at[taps_b, t_next], minus2)
        yield
        a.wait_recv()
        b.wait_recv()
        own_tiles, prev_tiles, next_tiles, far_tiles = (pl.ds(4 * i, 4) for i in (p, p_prev, p_next, p_far))
        a = put(mine.at[taps, own_tiles], mine.at[taps, own_tiles], plus)
        b = put(mine.at[taps, own_tiles], mine.at[taps, own_tiles], minus)
        across = [put(mine.at[taps, own_tiles], mine.at[taps, own_tiles], partner)]
        yield
        half_a, half_b = pl.ds(4 * p_prev, 2), pl.ds(4 * p_next + 2, 2)
        a.wait_recv()
        a = put(mine.at[taps, half_a], mine.at[taps, half_a], plus)
        b.wait_recv()
        b = put(mine.at[taps, half_b], mine.at[taps, half_b], minus)
        for tiles in (prev_tiles, next_tiles):
            across.append(put(mine.at[taps, tiles], mine.at[taps, tiles], partner))
        yield
        a.wait_recv()
        b.wait_recv()
        across.append(put(mine.at[taps, far_tiles], mine.at[taps, far_tiles], partner))
        yield
        for copy in across:
            copy.wait_recv()

    def finish_forward():
        for copy in halo2[:4]:
            copy.wait_recv()
        near_columns(ext2, 0)
        block_ref[...] = clip_ref[...] + convolve(0, 1, False)

    def finish_backward():
        for copy in halo2[4:]:
            copy.wait_recv()
        near_columns(ext2, 1)
        gclip_ref[...] = cot_ref[...] + convolve(1, 0, True)

    running = [stream(*one) for one in STREAMS]

    def advance(*which):
        for n in which:
            next(running[n], None)

    advance(0, 1, 0, 2, 1, 3)
    halo2 += to_others(ext2, inner)
    advance(2, 3, 0, 1)
    advance(0, 1, 2, 3)
    finish_forward()
    advance(0, 1, 2, 3)
    finish_backward()
    for _ in range(12):
        advance(0, 1, 2, 3)
    for copy in started:
        copy.wait_send()


def per_device(clip, kernel_one, kernel_two, cotangent):
    vmem = pl.BlockSpec(memory_space=pltpu.VMEM)
    anywhere = pl.BlockSpec(memory_space=pl.ANY)
    field = jax.ShapeDtypeStruct(clip.shape, F32)
    block_out, grad_clip, sums = pl.pallas_call(
        kernel,
        out_shape=(field, field, jax.ShapeDtypeStruct((2, 32, 16, 8, 128), F32)),
        in_specs=[vmem, vmem, anywhere, anywhere],
        out_specs=(vmem, vmem, vmem),
        scratch_shapes=[
            pltpu.VMEM((2, 27, 128, 128), F32),
            pltpu.VMEM((2, 27, 128, 128), BF16),
            pltpu.VMEM((2, 27, 128, 128), BF16),
            pltpu.VMEM((2, 6, 6, 32, 128), F32),
            pltpu.VMEM((2, 6, 6, 32, 128), F32),
            pltpu.VMEM((2, 2, 3, 6, 6, 32, 128), BF16),
            pltpu.VMEM((512, 256), F32),
            pltpu.VMEM((4, 2, 32, 128), F32),
            pltpu.VMEM((256, 512), BF16),
            pltpu.VMEM((32, 16, 8, 128), F32),
            pltpu.VMEM((2, 27, 2, 8, 128), F32),
            pltpu.VMEM((2, 27, 4, 8, 128), F32),
            pltpu.VMEM((2, 27, 8, 128), F32),
            pltpu.VMEM((2, 27, 8, 128), F32),
            pltpu.VMEM((4, 8, 8, 128), F32),
            pltpu.SemaphoreType.DMA((COPIES,)),
            pltpu.SemaphoreType.DMA((COPIES,)),
            pltpu.SemaphoreType.DMA((2,)),
        ],
        compiler_params=pltpu.CompilerParams(
            collective_id=0, has_side_effects=True, vmem_limit_bytes=48 * 1024 * 1024
        ),
        cost_estimate=pl.CostEstimate(flops=6 * 4 * 226492416, bytes_accessed=8 * 1024 * 1024, transcendentals=32768),
    )(clip, cotangent, kernel_one.reshape(27, 128, 128), kernel_two.reshape(27, 128, 128))
    grad_two, grad_one = (sums[n, :27].reshape(kernel_one.shape) for n in range(2))
    return block_out, grad_clip, grad_one, grad_two


def solution(mesh):
    field = P("tm", "rows", None, None)
    return jax.shard_map(
        per_device,
        mesh=mesh,
        in_specs=(field, P(), P(), field),
        out_specs=(field, field, P(), P()),
        check_vma=False,
    )
```

```python
import jax
import jax.numpy as jnp
from jax import lax
from jax.experimental import pallas as pl
from jax.experimental.pallas import tpu as pltpu
from jax.sharding import PartitionSpec as P

MESH = pl.DeviceIdType.MESH
F32 = jnp.float32
BF16 = jnp.bfloat16
TAPS = [(a, b, c) for a in range(3) for b in range(3) for c in range(3)]
GROUPS = [TAPS[0:8], TAPS[8:16], TAPS[16:24], TAPS[24:27]]
STREAMS = [(0, 4, True), (4, 4, False), (8, 4, True), (12, 3, False), (15, 3, True), (18, 3, False), (21, 3, True), (24, 3, False)]
PHASES = (0.0, 4.9, 8.4, 13.4, 18.4, 22.0, 27.0, 28.0)
STEP = 1.9
COPIES = 320
Q = 1.0 / 256.0


def tap_index(tap):
    return (tap[0] * 3 + tap[1]) * 3 + tap[2]


def split(v):
    hi = v.astype(BF16)
    return hi, (v - hi.astype(F32)).astype(BF16)


def kernel(
    clip_ref, cot_ref, k1_ref, k2_ref,
    block_ref, gclip_ref, sums,
    kf, kh, kl, ext, ext2, cols, acc, pre, fixed, part, r1, r2, rz,
    send_sem, recv_sem, load_sem,
):
    tm = lax.axis_index("tm")
    rows = lax.axis_index("rows")
    x, z = lax.rem(tm, 4), lax.div(tm, 4)
    core, y = lax.rem(rows, 2), lax.div(rows, 2)

    def at(xx, yy, zz):
        return (zz * 4 + lax.rem(xx, 4), lax.rem(yy, 4) * 2 + core)

    partner_row = y * 2 + 1 - core
    outer_row = lax.rem(rows + 2 * core - 1 + 8, 8)
    tm_next, tm_prev = lax.rem(tm + 1, 32), lax.rem(tm + 31, 32)
    partner = (tm, partner_row)
    own = pl.ds(1 + 2 * core, 2)

    loads = []
    for src, dst in ((clip_ref, ext.at[0, 2:6, own]), (cot_ref, ext.at[1, 0:4, own]), (k1_ref, kf.at[0]), (k2_ref, kf.at[1])):
        loads.append(pltpu.make_async_copy(src, dst, load_sem.at[len(loads)]))
        loads[-1].start()

    peers = [partner, (tm, outer_row)]
    for t in (tm_next, tm_prev):
        peers += [(t, rows), (t, partner_row), (t, outer_row)]
    for d in range(1, 4):
        peers += [at(x + d, y, z), at(x, y + d, z)]
    peers += [at(x, y, lax.rem(z + d, 8)) for d in range(1, 8)]
    barrier = pltpu.get_barrier_semaphore()
    for peer in peers:
        pl.semaphore_signal(barrier, inc=1, device_id=peer, device_id_type=MESH)
    for load in loads[:2]:
        load.wait()
    pl.semaphore_wait(barrier, len(peers))

    started = []

    def put(src, dst, device, sends=None):
        n = len(started)
        copy = pltpu.make_async_remote_copy(
            src_ref=src, dst_ref=dst, send_sem=send_sem.at[n], recv_sem=recv_sem.at[n],
            device_id=device, device_id_type=MESH,
        )
        if sends is None:
            copy.start()
        else:
            pl.when(sends)(copy.start)
        started.append((copy, sends))
        return copy

    edge, edge_there, inner = 1 + 3 * core, 5 - 5 * core, 2 + core
    sides = ((0, pl.ds(2, 4), pl.ds(4, 2), pl.ds(0, 2), tm_next), (1, pl.ds(0, 4), pl.ds(0, 2), pl.ds(4, 2), tm_prev))

    def to_partner(field):
        return [put(field.at[n, mine, own], field.at[n, mine, own], partner) for n, mine, _, _, _ in sides]

    def to_others(field):
        out = []
        for n, mine, src, dst, there in sides:
            out.append(put(field.at[n, src, own], field.at[n, dst, own], (there, rows)))
            out.append(put(field.at[n, mine, edge], field.at[n, mine, edge_there], (tm, outer_row)))
            out.append(put(field.at[n, src, edge], field.at[n, dst, edge_there], (there, outer_row)))
            out.append(put(field.at[n, src, inner], field.at[n, dst, inner], (there, partner_row)))
        return out

    halo = to_others(ext)
    beside = to_partner(ext)

    for load in loads[2:]:
        load.wait()

    def split_tap(t, _):
        for n in range(2):
            kh[n, t], kl[n, t] = split(kf[n, t])
        return 0

    lax.fori_loop(0, 27, split_tap, 0)
    for copy in halo + beside:
        copy.wait_recv()
    halo_frames, own_frames = pl.ds(4 * core, 2), pl.ds(2 - 2 * core, 4)
    outer_rows = pl.ds(4 * core, 2)
    passed = [
        put(ext.at[core, halo_frames, outer_rows], ext.at[core, halo_frames, outer_rows], partner),
        put(ext.at[core, own_frames, 5 * core], ext.at[core, own_frames, 5 * core], partner),
    ]

    at_column = lax.broadcasted_iota(jnp.int32, (32, 128), 0)

    def columns(field, n, row):
        inside = jnp.logical_not(((row == 0) & (y == 0)) | ((row == 5) & (y == 3)))
        for f in range(6):
            keep = inside
            if n == 0 and f < 2:
                keep = keep & (tm > 0)
            if n == 1 and f > 3:
                keep = keep & (tm < 31)
            v = jnp.where(keep, field[n, f, row], 0.0)
            hi = v.astype(BF16).astype(F32)
            lo = v - hi
            for h, piece in enumerate((hi, lo)):
                cols[n, h, 0, f, row] = jnp.where(at_column == 0, 0.0, pltpu.roll(piece, 1, 0)).astype(BF16)
                cols[n, h, 1, f, row] = piece.astype(BF16)
                cols[n, h, 2, f, row] = jnp.where(at_column == 31, 0.0, pltpu.roll(piece, 31, 0)).astype(BF16)

    def convolve(n, kernel_at, turned):
        for g, group in enumerate(GROUPS):
            left, right = [], []
            for a, b, c in group:
                at_tap = tap_index((a, b, c))
                i, j, k = (2 - a, 2 - b, 2 - c) if turned else (a, b, c)
                window = [cols[n, h, k, i : i + 4, pl.ds(2 * core + j, 2)].reshape(256, 128) for h in range(2)]
                left.append(jnp.concatenate(window, 0))
                right.append(jnp.concatenate([kh[kernel_at, at_tap], kl[kernel_at, at_tap]], 0 if turned else 1))
            left = jnp.concatenate(left, 1)
            right = jnp.concatenate(right, 1 if turned else 0)
            product = lax.dot_general(left, right, (((1,), (1 if turned else 0,)), ((), ())), preferred_element_type=F32)
            if g == 0:
                acc[...] = product
            else:
                acc[...] += product
            yield

    def convolved():
        total = acc[0:256, 0:128] + (acc[0:256, 128:256] + acc[256:512, 0:128]) + acc[256:512, 128:256]
        return total.reshape(4, 2, 32, 128)

    def near_columns(field, n):
        def one(j, _):
            columns(field, n, 2 * core + j)
            return 0

        lax.fori_loop(0, 4, one, 0)

    near_columns(ext, 0)
    for _ in convolve(0, 0, False):
        pass
    pre[...] = convolved()
    near_columns(ext, 1)
    for _ in convolve(1, 1, True):
        pass
    v = pre[...]
    s = jax.nn.sigmoid(v)
    ext2[0, 2:6, own] = v * s
    ext2[1, 0:4, own] = convolved() * s * (1.0 + v * (1.0 - s))
    swap = to_partner(ext2)

    for copy in passed:
        copy.wait_recv()

    @pl.when(core == 0)
    def _():
        for row in (4, 5):
            columns(ext, 1, row)

    @pl.when(core == 1)
    def _():
        for row in (0, 1):
            columns(ext, 0, row)

    for copy in swap:
        copy.wait_recv()
    whole = ext2[core, own_frames, 1:5].reshape(512, 128)
    fixed[0:128], fixed[128:256] = split(whole.T)

    def gradient(tap):
        a, b, c = (core * t + (1 - core) * (2 - t) for t in tap)
        right = [cols[1 - core, h, c, pl.ds(a, 4), pl.ds(b, 4)].reshape(512, 128) for h in range(2)]
        m = jnp.dot(fixed[...], jnp.concatenate(right, 1), preferred_element_type=F32)
        m = m[0:128, 0:128] + (m[0:128, 128:256] + m[128:256, 0:128]) + m[128:256, 128:256]
        part[tap_index(tap)] = jnp.where(core == 1, m.T, m).reshape(16, 8, 128)

    def stream(which, first, count, x_first):
        taps = pl.ds(first, count)
        rings = [[at(x + d, y, z) for d in (1, 2, 3)], [at(x, y + d, z) for d in (1, 2, 3)]]
        p, s = (x, y) if x_first else (y, x)
        ring, ring2 = rings if x_first else rings[::-1]
        p_of, s_of = ([lax.rem(i + d, 4) for d in range(4)] for i in (p, s))
        tile = 4 * p + s
        mine = sums.at[core]
        place = [lax.rem(z + d + 64 - first, 8) for d in range(8)]
        owns = [k < count for k in place]
        tap_at = [first + lax.rem(k, count) for k in place]
        z_of = [lax.rem(z + d, 8) for d in range(8)]

        def same(ref, to):
            return put(ref, ref, to)

        for tap in TAPS[first : first + count]:
            gradient(tap)
        sent = [put(part.at[taps, pl.ds(4 * p_of[d], 4)], r1.at[d - 1, taps], ring[d - 1]) for d in (1, 2, 3)]
        yield
        for copy in sent:
            copy.wait_recv()
        part[taps, pl.ds(4 * p, 4)] += r1[0, taps] + r1[1, taps] + r1[2, taps]
        sent = [put(part.at[taps, 4 * p + s_of[d]], r2.at[d - 1, taps], ring2[d - 1]) for d in (1, 2, 3)]
        yield
        for copy in sent:
            copy.wait_recv()
        part[taps, tile] += r2[0, taps] + r2[1, taps] + r2[2, taps]
        sent = []
        for d in range(1, 8):
            sent.append(put(part.at[tap_at[d], tile], rz.at[which, d - 1], at(x, y, z_of[d]), owns[d]))
        yield

        @pl.when(owns[0])
        def _():
            total = part[tap_at[0], tile]
            for d in range(1, 8):
                sent[d - 1].wait_recv()
                total = total + rz[which, d - 1]
            mine[tap_at[0], tile] = total * Q

        done = mine.at[tap_at[0], tile]
        sent = [put(done, done, at(x, y, z_of[d]), owns[0]) for d in range(1, 8)]
        yield
        for d in range(1, 8):
            pl.when(owns[8 - d])(sent[d - 1].wait_recv)
        sent = [same(mine.at[taps, tile], to) for to in ring2]
        yield
        for copy in sent:
            copy.wait_recv()
        sent = [same(mine.at[taps, pl.ds(4 * p, 4)], to) for to in ring]
        across = [same(mine.at[taps, pl.ds(4 * p, 4)], partner)]
        yield
        for d in (1, 2, 3):
            sent[d - 1].wait_recv()
            across.append(same(mine.at[taps, pl.ds(4 * p_of[4 - d], 4)], partner))
        yield
        for copy in across:
            copy.wait_recv()

    def finish():
        for n, field, out, kernel_at, own_frames in ((0, ext, block_ref, 1, pl.ds(2, 4)), (1, ext, gclip_ref, 0, pl.ds(0, 4))):
            for copy in halo2[4 * n : 4 * n + 4]:
                copy.wait_recv()
            near_columns(ext2, n)
            yield
            yield from convolve(n, kernel_at, n == 1)
            out[...] = field[n, own_frames, own] + convolved()
            yield

    running = [stream(n, *one) for n, one in enumerate(STREAMS)]
    finishing = finish()
    order = []
    for n in range(len(STREAMS)):
        for phase, start in enumerate(PHASES):
            order.append(((n // 2) * (STEP if phase else 0.6) + start, phase, n))
    halo2 = []
    for when, phase, n in sorted(order):
        if phase and not halo2:
            halo2 += to_others(ext2)
        next(running[n], None)
        if when > 6.0 and n % 2:
            next(finishing, None)
    for _ in finishing:
        pass
    for copy, sends in started:
        if sends is None:
            copy.wait_send()
        else:
            pl.when(sends)(copy.wait_send)


def copy_out(block_ref, gclip_ref, sums, block_out, gclip_out, one_out, two_out, sem):
    copies = []
    for src, dst in ((sums.at[1], one_out), (sums.at[0], two_out), (block_ref, block_out), (gclip_ref, gclip_out)):
        copies.append(pltpu.make_async_copy(src, dst, sem.at[len(copies)]))
        copies[-1].start()
    for copy in copies:
        copy.wait()


def per_device(clip, kernel_one, kernel_two, cotangent):
    vmem = pl.BlockSpec(memory_space=pltpu.VMEM)
    hbm = pl.BlockSpec(memory_space=pltpu.HBM)
    anywhere = pl.BlockSpec(memory_space=pl.ANY)
    field = jax.ShapeDtypeStruct(clip.shape, F32)
    block_out, grad_clip, sums = pl.pallas_call(
        kernel,
        out_shape=(field, field, jax.ShapeDtypeStruct((2, 27, 16, 8, 128), F32)),
        in_specs=[hbm] * 4,
        out_specs=(vmem, vmem, vmem),
        scratch_shapes=[
            pltpu.VMEM((2, 27, 128, 128), F32),
            pltpu.VMEM((2, 27, 128, 128), BF16),
            pltpu.VMEM((2, 27, 128, 128), BF16),
            pltpu.VMEM((2, 6, 6, 32, 128), F32),
            pltpu.VMEM((2, 6, 6, 32, 128), F32),
            pltpu.VMEM((2, 2, 3, 6, 6, 32, 128), BF16),
            pltpu.VMEM((512, 256), F32),
            pltpu.VMEM((4, 2, 32, 128), F32),
            pltpu.VMEM((256, 512), BF16),
            pltpu.VMEM((27, 16, 8, 128), F32),
            pltpu.VMEM((3, 27, 4, 8, 128), F32),
            pltpu.VMEM((3, 27, 8, 128), F32),
            pltpu.VMEM((len(STREAMS), 7, 8, 128), F32),
            pltpu.SemaphoreType.DMA((COPIES,)),
            pltpu.SemaphoreType.DMA((COPIES,)),
            pltpu.SemaphoreType.DMA((4,)),
        ],
        compiler_params=pltpu.CompilerParams(
            collective_id=0, has_side_effects=True, vmem_limit_bytes=32 * 1024 * 1024
        ),
        cost_estimate=pl.CostEstimate(flops=6 * 4 * 226492416, bytes_accessed=8 * 1024 * 1024, transcendentals=32768),
    )(clip, cotangent, kernel_one.reshape(27, 128, 128), kernel_two.reshape(27, 128, 128))
    grad = jax.ShapeDtypeStruct((27, 16, 8, 128), F32)
    block_out, grad_clip, grad_one, grad_two = pl.pallas_call(
        copy_out,
        out_shape=(field, field, grad, grad),
        in_specs=[anywhere] * 3,
        out_specs=(hbm,) * 4,
        scratch_shapes=[pltpu.SemaphoreType.DMA((4,))],
        compiler_params=pltpu.CompilerParams(vmem_limit_bytes=1024 * 1024),
        cost_estimate=pl.CostEstimate(flops=0, bytes_accessed=8 * 1024 * 1024, transcendentals=0),
    )(block_out, grad_clip, sums)
    return block_out, grad_clip, grad_one.reshape(kernel_one.shape), grad_two.reshape(kernel_two.shape)


def solution(mesh):
    field = P("tm", "rows", None, None)
    return jax.shard_map(
        per_device,
        mesh=mesh,
        in_specs=(field, P(), P(), field),
        out_specs=(field, field, P(), P()),
        check_vma=False,
    )
```

```python
import jax
import jax.numpy as jnp
from jax import lax
from jax.experimental import pallas as pl
from jax.experimental.pallas import tpu as pltpu
from jax.sharding import PartitionSpec as P

MESH = pl.DeviceIdType.MESH
F32 = jnp.float32
BF16 = jnp.bfloat16
TAPS = [(a, b, c) for a in range(3) for b in range(3) for c in range(3)]
GROUPS = [TAPS[0:8], TAPS[8:16], TAPS[16:24], TAPS[24:27]]
STREAMS = []


def plan():
    first = 0
    for k, (along_x, along_y) in enumerate(((3, 3), (3, 3), (3, 2), (2, 2))):
        begin = (0.1, 0.3, 5.7, 7.7)[k]
        arrive = 0.6 + 1.9 * (k + 1) + 3.0
        late = [arrive + t for t in (0.0, 3.8, 8.8, 13.8, 17.6, 22.8, 23.8)]
        for n, (axis, count) in enumerate((("x", along_x), ("y", along_y))):
            STREAMS.append((first, count, axis, [0.05 * n + t for t in [0.2 * k, begin] + late]))
            first += count
    for k in range(2):
        STREAMS.append((first, 3, "z", [0.35 + 0.25 * k + t for t in (0.0, 0.1, 8.0 + 3.0 * k, 13.0 + 3.0 * k, 18.0 + 3.0 * k, 26.0 + 3.0 * k, 27.0 + 3.0 * k)]))
        first += 3


plan()
COPIES = 400
Q = 1.0 / 256.0


def tap_index(tap):
    return (tap[0] * 3 + tap[1]) * 3 + tap[2]


def split(v):
    hi = v.astype(BF16)
    return hi, (v - hi.astype(F32)).astype(BF16)


def kernel(
    clip_ref, cot_ref, k1_ref, k2_ref,
    block_ref, gclip_ref, sums,
    kf, kh, kl, ext, ext2, cols, acc, pre, fixed, part, r1, r2, rz, c1, c2,
    send_sem, recv_sem, load_sem,
):
    tm = lax.axis_index("tm")
    rows = lax.axis_index("rows")
    x, z = lax.rem(tm, 4), lax.div(tm, 4)
    core, y = lax.rem(rows, 2), lax.div(rows, 2)

    def at(xx, yy, zz):
        return (zz * 4 + lax.rem(xx, 4), lax.rem(yy, 4) * 2 + core)

    partner_row = y * 2 + 1 - core
    outer_row = lax.rem(rows + 2 * core - 1 + 8, 8)
    tm_next, tm_prev = lax.rem(tm + 1, 32), lax.rem(tm + 31, 32)
    partner = (tm, partner_row)
    own = pl.ds(1 + 2 * core, 2)

    loads = []
    for src, dst in ((clip_ref, ext.at[0, 2:6, own]), (cot_ref, ext.at[1, 0:4, own]), (k1_ref, kf.at[0]), (k2_ref, kf.at[1])):
        loads.append(pltpu.make_async_copy(src, dst, load_sem.at[len(loads)]))
        loads[-1].start()

    peers = [partner, (tm, outer_row)]
    for t in (tm_next, tm_prev):
        peers += [(t, rows), (t, partner_row), (t, outer_row)]
    plane = [(d % 4, d // 4) for d in range(1, 16)]
    peers += [at(x + dx, y + dy, z) for dx, dy in plane]
    peers += [at(x, y, lax.rem(z + d, 8)) for d in range(1, 8)]
    barrier = pltpu.get_barrier_semaphore()
    for peer in peers:
        pl.semaphore_signal(barrier, inc=1, device_id=peer, device_id_type=MESH)
    for load in loads[:2]:
        load.wait()
    pl.semaphore_wait(barrier, len(peers))

    started = []

    def put(src, dst, device, sends=None):
        n = len(started)
        copy = pltpu.make_async_remote_copy(
            src_ref=src, dst_ref=dst, send_sem=send_sem.at[n], recv_sem=recv_sem.at[n],
            device_id=device, device_id_type=MESH,
        )
        if sends is None:
            copy.start()
        else:
            pl.when(sends)(copy.start)
        started.append((copy, sends))
        return copy

    edge, edge_there, inner = 1 + 3 * core, 5 - 5 * core, 2 + core
    sides = ((0, pl.ds(2, 4), pl.ds(4, 2), pl.ds(0, 2), tm_next), (1, pl.ds(0, 4), pl.ds(0, 2), pl.ds(4, 2), tm_prev))

    def to_partner(field):
        return [put(field.at[n, mine, own], field.at[n, mine, own], partner) for n, mine, _, _, _ in sides]

    def to_others(field):
        out = []
        for n, mine, src, dst, there in sides:
            out.append(put(field.at[n, src, own], field.at[n, dst, own], (there, rows)))
            out.append(put(field.at[n, mine, edge], field.at[n, mine, edge_there], (tm, outer_row)))
            out.append(put(field.at[n, src, edge], field.at[n, dst, edge_there], (there, outer_row)))
            out.append(put(field.at[n, src, inner], field.at[n, dst, inner], (there, partner_row)))
        return out

    halo = to_others(ext)
    beside = to_partner(ext)

    for load in loads[2:]:
        load.wait()

    def split_tap(t, _):
        for n in range(2):
            kh[n, t], kl[n, t] = split(kf[n, t])
        return 0

    lax.fori_loop(0, 27, split_tap, 0)
    for copy in halo + beside:
        copy.wait_recv()
    halo_frames, own_frames = pl.ds(4 * core, 2), pl.ds(2 - 2 * core, 4)
    outer_rows = pl.ds(4 * core, 2)
    passed = [
        put(ext.at[core, halo_frames, outer_rows], ext.at[core, halo_frames, outer_rows], partner),
        put(ext.at[core, own_frames, 5 * core], ext.at[core, own_frames, 5 * core], partner),
    ]

    at_column = lax.broadcasted_iota(jnp.int32, (32, 128), 0)

    def columns(field, n, row):
        inside = jnp.logical_not(((row == 0) & (y == 0)) | ((row == 5) & (y == 3)))
        for f in range(6):
            keep = inside
            if n == 0 and f < 2:
                keep = keep & (tm > 0)
            if n == 1 and f > 3:
                keep = keep & (tm < 31)
            v = jnp.where(keep, field[n, f, row], 0.0)
            hi = v.astype(BF16).astype(F32)
            lo = v - hi
            for h, piece in enumerate((hi, lo)):
                cols[n, h, 0, f, row] = jnp.where(at_column == 0, 0.0, pltpu.roll(piece, 1, 0)).astype(BF16)
                cols[n, h, 1, f, row] = piece.astype(BF16)
                cols[n, h, 2, f, row] = jnp.where(at_column == 31, 0.0, pltpu.roll(piece, 31, 0)).astype(BF16)

    def convolve(n, kernel_at, turned):
        for g, group in enumerate(GROUPS):
            left, right = [], []
            for a, b, c in group:
                at_tap = tap_index((a, b, c))
                i, j, k = (2 - a, 2 - b, 2 - c) if turned else (a, b, c)
                window = [cols[n, h, k, i : i + 4, pl.ds(2 * core + j, 2)].reshape(256, 128) for h in range(2)]
                left.append(jnp.concatenate(window, 0))
                right.append(jnp.concatenate([kh[kernel_at, at_tap], kl[kernel_at, at_tap]], 0 if turned else 1))
            left = jnp.concatenate(left, 1)
            right = jnp.concatenate(right, 1 if turned else 0)
            product = lax.dot_general(left, right, (((1,), (1 if turned else 0,)), ((), ())), preferred_element_type=F32)
            if g == 0:
                acc[...] = product
            else:
                acc[...] += product
            yield

    def convolved():
        total = acc[0:256, 0:128] + (acc[0:256, 128:256] + acc[256:512, 0:128]) + acc[256:512, 128:256]
        return total.reshape(4, 2, 32, 128)

    def near_columns(field, n):
        def one(j, _):
            columns(field, n, 2 * core + j)
            return 0

        lax.fori_loop(0, 4, one, 0)

    near_columns(ext, 0)
    for _ in convolve(0, 0, False):
        pass
    pre[...] = convolved()
    near_columns(ext, 1)
    for _ in convolve(1, 1, True):
        pass
    v = pre[...]
    s = jax.nn.sigmoid(v)
    ext2[0, 2:6, own] = v * s
    ext2[1, 0:4, own] = convolved() * s * (1.0 + v * (1.0 - s))
    swap = to_partner(ext2)

    for copy in passed:
        copy.wait_recv()

    @pl.when(core == 0)
    def _():
        for row in (4, 5):
            columns(ext, 1, row)

    @pl.when(core == 1)
    def _():
        for row in (0, 1):
            columns(ext, 0, row)

    for copy in swap:
        copy.wait_recv()
    whole = ext2[core, own_frames, 1:5].reshape(512, 128)
    fixed[0:128], fixed[128:256] = split(whole.T)

    def gradient(tap):
        a, b, c = (core * t + (1 - core) * (2 - t) for t in tap)
        right = [cols[1 - core, h, c, pl.ds(a, 4), pl.ds(b, 4)].reshape(512, 128) for h in range(2)]
        m = jnp.dot(fixed[...], jnp.concatenate(right, 1), preferred_element_type=F32)
        m = m[0:128, 0:128] + (m[0:128, 128:256] + m[128:256, 0:128]) + m[128:256, 128:256]
        part[tap_index(tap)] = jnp.where(core == 1, m.T, m).reshape(16, 8, 128)

    def stream(which, first, count, x_first):
        taps = pl.ds(first, count)
        rings = [[at(x + d, y, z) for d in (1, 2, 3)], [at(x, y + d, z) for d in (1, 2, 3)]]
        p, s = (x, y) if x_first else (y, x)
        ring, ring2 = rings if x_first else rings[::-1]
        p_of, s_of = ([lax.rem(i + d, 4) for d in range(4)] for i in (p, s))
        tile = 4 * p + s
        mine = sums.at[core]
        place = [lax.rem(z + d + 64 - first, 8) for d in range(8)]
        owns = [k < count for k in place]
        tap_at = [first + lax.rem(k, count) for k in place]
        z_of = [lax.rem(z + d, 8) for d in range(8)]

        def same(ref, to):
            return put(ref, ref, to)

        for tap in TAPS[first : first + count]:
            gradient(tap)
        yield
        sent = [put(part.at[taps, pl.ds(4 * p_of[d], 4)], r1.at[d - 1, taps], ring[d - 1]) for d in (1, 2, 3)]
        yield
        for copy in sent:
            copy.wait_recv()
        part[taps, pl.ds(4 * p, 4)] += r1[0, taps] + r1[1, taps] + r1[2, taps]
        sent = [put(part.at[taps, 4 * p + s_of[d]], r2.at[d - 1, taps], ring2[d - 1]) for d in (1, 2, 3)]
        yield
        for copy in sent:
            copy.wait_recv()
        part[taps, tile] += r2[0, taps] + r2[1, taps] + r2[2, taps]
        sent = []
        for d in range(1, 8):
            sent.append(put(part.at[tap_at[d], tile], rz.at[which, d - 1], at(x, y, z_of[d]), owns[d]))
        yield

        @pl.when(owns[0])
        def _():
            total = part[tap_at[0], tile]
            for d in range(1, 8):
                sent[d - 1].wait_recv()
                total = total + rz[which, d - 1]
            mine[tap_at[0], tile] = total * Q

        done = mine.at[tap_at[0], tile]
        sent = [put(done, done, at(x, y, z_of[d]), owns[0]) for d in range(1, 8)]
        yield
        for d in range(1, 8):
            pl.when(owns[8 - d])(sent[d - 1].wait_recv)
        sent = [same(mine.at[taps, tile], to) for to in ring2]
        yield
        for copy in sent:
            copy.wait_recv()
        sent = [same(mine.at[taps, pl.ds(4 * p, 4)], to) for to in ring]
        across = [same(mine.at[taps, pl.ds(4 * p, 4)], partner)]
        yield
        for d in (1, 2, 3):
            sent[d - 1].wait_recv()
            across.append(same(mine.at[taps, pl.ds(4 * p_of[4 - d], 4)], partner))
        yield
        for copy in across:
            copy.wait_recv()

    def stream_z(which, first, count):
        taps = pl.ds(first, count)
        got = pl.ds((which - 8) * count, count)
        z_of = [lax.rem(z + d, 8) for d in range(8)]
        mine = sums.at[core]

        def owned(xx, yy):
            o = lax.rem(lax.rem(xx, 4) + 4 * lax.rem(yy, 4) + 64 - 6 * (which - 8), 16)
            return o < 2 * count, first + lax.rem(lax.div(o, 2), count), 2 * z + lax.rem(o, 2)

        for tap in TAPS[first : first + count]:
            gradient(tap)
        yield
        sent = [put(part.at[taps, pl.ds(2 * z_of[d], 2)], c1.at[d - 1, got], at(x, y, z_of[d])) for d in range(1, 8)]
        yield
        total = part[taps, pl.ds(2 * z, 2)]
        for d in range(1, 8):
            sent[d - 1].wait_recv()
            total = total + c1[d - 1, got]
        part[taps, pl.ds(2 * z, 2)] = total
        sent = []
        for n, (dx, dy) in enumerate(plane):
            owns, tap, tile = owned(x + dx, y + dy)
            sent.append(put(part.at[tap, tile], c2.at[which - 8, n], at(x + dx, y + dy, z), owns))
        yield
        owns, tap, tile = owned(x, y)

        @pl.when(owns)
        def _():
            total = part[tap, tile]
            for n in range(15):
                sent[n].wait_recv()
                total = total + c2[which - 8, n]
            mine[tap, tile] = total * Q

        done = mine.at[tap, tile]
        sent = [put(done, done, at(x + dx, y + dy, z), owns) for dx, dy in plane]
        yield
        for n, (dx, dy) in enumerate(plane):
            pl.when(owned(x + 4 - dx, y + 4 - dy)[0])(sent[n].wait_recv)
        done = mine.at[taps, pl.ds(2 * z, 2)]
        sent = [put(done, done, at(x, y, z_of[d])) for d in range(1, 8)]
        across = [put(done, done, partner)]
        yield
        for d in range(1, 8):
            sent[d - 1].wait_recv()
            done = mine.at[taps, pl.ds(2 * z_of[8 - d], 2)]
            across.append(put(done, done, partner))
        yield
        for copy in across:
            copy.wait_recv()

    def finish():
        for n, field, out, kernel_at, own_frames in ((0, ext, block_ref, 1, pl.ds(2, 4)), (1, ext, gclip_ref, 0, pl.ds(0, 4))):
            for copy in halo2[4 * n : 4 * n + 4]:
                copy.wait_recv()
            near_columns(ext2, n)
            yield
            yield from convolve(n, kernel_at, n == 1)
            out[...] = field[n, own_frames, own] + convolved()
            yield

    running, order = [], []
    for n, (first, count, axis, times) in enumerate(STREAMS):
        running.append(stream_z(n, first, count) if axis == "z" else stream(n, first, count, axis == "x"))
        order += [(time, n) for time in times]
    finishing = finish()
    halo2 = []
    for time, n in sorted(order):
        if time > 5.9 and not halo2:
            halo2 += to_others(ext2)
        next(running[n], None)
        if time > 11.0:
            next(finishing, None)
    for _ in finishing:
        pass
    for copy, sends in started:
        if sends is None:
            copy.wait_send()
        else:
            pl.when(sends)(copy.wait_send)


def copy_out(block_ref, gclip_ref, sums, block_out, gclip_out, one_out, two_out, sem):
    copies = []
    pieces = [(block_ref, block_out), (gclip_ref, gclip_out)]
    for n, out in ((1, one_out), (0, two_out)):
        pieces += [(sums.at[n, pl.ds(9 * i, 9)], out.at[pl.ds(9 * i, 9)]) for i in range(3)]
    for src, dst in pieces:
        copies.append(pltpu.make_async_copy(src, dst, sem.at[len(copies)]))
        copies[-1].start()
    for copy in copies:
        copy.wait()


def per_device(clip, kernel_one, kernel_two, cotangent):
    vmem = pl.BlockSpec(memory_space=pltpu.VMEM)
    hbm = pl.BlockSpec(memory_space=pltpu.HBM)
    anywhere = pl.BlockSpec(memory_space=pl.ANY)
    field = jax.ShapeDtypeStruct(clip.shape, F32)
    block_out, grad_clip, sums = pl.pallas_call(
        kernel,
        out_shape=(field, field, jax.ShapeDtypeStruct((2, 27, 16, 8, 128), F32)),
        in_specs=[hbm] * 4,
        out_specs=(vmem, vmem, vmem),
        scratch_shapes=[
            pltpu.VMEM((2, 27, 128, 128), F32),
            pltpu.VMEM((2, 27, 128, 128), BF16),
            pltpu.VMEM((2, 27, 128, 128), BF16),
            pltpu.VMEM((2, 6, 6, 32, 128), F32),
            pltpu.VMEM((2, 6, 6, 32, 128), F32),
            pltpu.VMEM((2, 2, 3, 6, 6, 32, 128), BF16),
            pltpu.VMEM((512, 256), F32),
            pltpu.VMEM((4, 2, 32, 128), F32),
            pltpu.VMEM((256, 512), BF16),
            pltpu.VMEM((27, 16, 8, 128), F32),
            pltpu.VMEM((3, 27, 4, 8, 128), F32),
            pltpu.VMEM((3, 27, 8, 128), F32),
            pltpu.VMEM((8, 7, 8, 128), F32),
            pltpu.VMEM((7, 6, 2, 8, 128), F32),
            pltpu.VMEM((2, 15, 8, 128), F32),
            pltpu.SemaphoreType.DMA((COPIES,)),
            pltpu.SemaphoreType.DMA((COPIES,)),
            pltpu.SemaphoreType.DMA((4,)),
        ],
        compiler_params=pltpu.CompilerParams(
            collective_id=0, has_side_effects=True, vmem_limit_bytes=32 * 1024 * 1024
        ),
        cost_estimate=pl.CostEstimate(flops=6 * 4 * 226492416, bytes_accessed=8 * 1024 * 1024, transcendentals=32768),
    )(*(pltpu.with_memory_space_constraint(a, pltpu.HBM) for a in (clip, cotangent, kernel_one.reshape(27, 128, 128), kernel_two.reshape(27, 128, 128))))
    grad = jax.ShapeDtypeStruct((27, 16, 8, 128), F32)
    block_out, grad_clip, grad_one, grad_two = pl.pallas_call(
        copy_out,
        out_shape=(field, field, grad, grad),
        in_specs=[anywhere] * 3,
        out_specs=(hbm,) * 4,
        scratch_shapes=[pltpu.SemaphoreType.DMA((8,))],
        compiler_params=pltpu.CompilerParams(vmem_limit_bytes=1024 * 1024),
        cost_estimate=pl.CostEstimate(flops=0, bytes_accessed=8 * 1024 * 1024, transcendentals=0),
    )(block_out, grad_clip, sums)
    return block_out, grad_clip, grad_one.reshape(kernel_one.shape), grad_two.reshape(kernel_two.shape)


def solution(mesh):
    field = P("tm", "rows", None, None)
    return jax.shard_map(
        per_device,
        mesh=mesh,
        in_specs=(field, P(), P(), field),
        out_specs=(field, field, P(), P()),
        check_vma=False,
    )
```

```python
import jax
import jax.numpy as jnp
from jax import lax
from jax.experimental import pallas as pl
from jax.experimental.pallas import tpu as pltpu
from jax.sharding import PartitionSpec as P

MESH = pl.DeviceIdType.MESH
F32 = jnp.float32
BF16 = jnp.bfloat16
TAPS = [(a, b, c) for a in range(3) for b in range(3) for c in range(3)]
GROUPS = [TAPS[0:8], TAPS[8:16], TAPS[16:24], TAPS[24:27]]
STREAMS = []


def plan():
    first = 0
    for k, (along_x, along_y) in enumerate(((3, 3), (3, 3), (3, 2), (2, 2))):
        begin = (0.1, 0.3, 5.7, 7.7)[k]
        arrive = 0.6 + 1.9 * (k + 1) + 3.0
        late = [arrive + t for t in (0.0, 3.8, 8.8, 13.8, 17.6, 22.8, 23.8)]
        for n, (axis, count) in enumerate((("x", along_x), ("y", along_y))):
            STREAMS.append((first, count, axis, [0.05 * n + t for t in [0.2 * k, begin] + late]))
            first += count
    for k in range(2):
        STREAMS.append((first, 3, "z", [0.35 + 0.25 * k + t for t in (0.0, 0.1, 8.0 + 3.0 * k, 13.0 + 3.0 * k, 18.0 + 3.0 * k, 26.0 + 3.0 * k, 27.0 + 3.0 * k)]))
        first += 3


plan()
COPIES = 400
Q = 1.0 / 256.0


def tap_index(tap):
    return (tap[0] * 3 + tap[1]) * 3 + tap[2]


def split(v):
    hi = v.astype(BF16)
    return hi, (v - hi.astype(F32)).astype(BF16)


def kernel(
    clip_ref, cot_ref, k1_ref, k2_ref,
    block_ref, gclip_ref, sums,
    kf, kh, kl, ext, ext2, cols, acc, pre, d_active, fixed, part, r1, r2, rz, c1, c2,
    send_sem, recv_sem, load_sem,
):
    tm = lax.axis_index("tm")
    rows = lax.axis_index("rows")
    x, z = lax.rem(tm, 4), lax.div(tm, 4)
    core, y = lax.rem(rows, 2), lax.div(rows, 2)

    def at(xx, yy, zz):
        return (zz * 4 + lax.rem(xx, 4), lax.rem(yy, 4) * 2 + core)

    partner_row = y * 2 + 1 - core
    outer_row = lax.rem(rows + 2 * core - 1 + 8, 8)
    tm_next, tm_prev = lax.rem(tm + 1, 32), lax.rem(tm + 31, 32)
    partner = (tm, partner_row)
    own = pl.ds(1 + 2 * core, 2)

    loads = []
    for src, dst in ((clip_ref, ext.at[0, 2:6, own]), (cot_ref, ext.at[1, 0:4, own]), (k1_ref, kf.at[0]), (k2_ref, kf.at[1])):
        loads.append(pltpu.make_async_copy(src, dst, load_sem.at[len(loads)]))
        loads[-1].start()

    peers = [partner, (tm, outer_row)]
    for t in (tm_next, tm_prev):
        peers += [(t, rows), (t, partner_row), (t, outer_row)]
    plane = [(d % 4, d // 4) for d in range(1, 16)]
    peers += [at(x + dx, y + dy, z) for dx, dy in plane]
    peers += [at(x, y, lax.rem(z + d, 8)) for d in range(1, 8)]
    barrier = pltpu.get_barrier_semaphore()
    for peer in peers:
        pl.semaphore_signal(barrier, inc=1, device_id=peer, device_id_type=MESH)
    for load in loads[:2]:
        load.wait()
    pl.semaphore_wait(barrier, len(peers))

    started = []

    def put(src, dst, device, sends=None):
        n = len(started)
        copy = pltpu.make_async_remote_copy(
            src_ref=src, dst_ref=dst, send_sem=send_sem.at[n], recv_sem=recv_sem.at[n],
            device_id=device, device_id_type=MESH,
        )
        if sends is None:
            copy.start()
        else:
            pl.when(sends)(copy.start)
        started.append((copy, sends))
        return copy

    edge, edge_there, inner = 1 + 3 * core, 5 - 5 * core, 2 + core
    sides = ((0, pl.ds(2, 4), pl.ds(4, 2), pl.ds(0, 2), tm_next), (1, pl.ds(0, 4), pl.ds(0, 2), pl.ds(4, 2), tm_prev))

    def to_partner(field):
        return [put(field.at[n, mine, own], field.at[n, mine, own], partner) for n, mine, _, _, _ in sides]

    def to_others(field):
        near, far = [], []
        for n, mine, _, _, _ in sides:
            near.append(put(field.at[n, mine, edge], field.at[n, mine, edge_there], (tm, outer_row)))
        for n, _, src, dst, there in sides:
            far.append([
                put(field.at[n, src, edge], field.at[n, dst, edge_there], (there, outer_row)),
                put(field.at[n, src, inner], field.at[n, dst, inner], (there, partner_row)),
                put(field.at[n, src, own], field.at[n, dst, own], (there, rows)),
            ])
        return near, far

    beside = to_partner(ext)
    near, far = to_others(ext)

    for load in loads[2:]:
        load.wait()

    def split_tap(t, _):
        for n in range(2):
            kh[n, t], kl[n, t] = split(kf[n, t])
        return 0

    lax.fori_loop(0, 27, split_tap, 0)
    at_column = lax.broadcasted_iota(jnp.int32, (32, 128), 0)

    def columns(field, n, row, frames):
        inside = jnp.logical_not(((row == 0) & (y == 0)) | ((row == 5) & (y == 3)))
        for f in frames:
            keep = inside
            if n == 0 and f < 2:
                keep = keep & (tm > 0)
            if n == 1 and f > 3:
                keep = keep & (tm < 31)
            v = jnp.where(keep, field[n, f, row], 0.0)
            hi = v.astype(BF16).astype(F32)
            lo = v - hi
            for h, piece in enumerate((hi, lo)):
                cols[n, h, 0, f, row] = jnp.where(at_column == 0, 0.0, pltpu.roll(piece, 1, 0)).astype(BF16)
                cols[n, h, 1, f, row] = piece.astype(BF16)
                cols[n, h, 2, f, row] = jnp.where(at_column == 31, 0.0, pltpu.roll(piece, 31, 0)).astype(BF16)

    def convolve(n, kernel_at, turned, first):
        for g, group in enumerate(GROUPS):
            left, right = [], []
            for a, b, c in group:
                at_tap = tap_index((a, b, c))
                i, j, k = (2 - a, 2 - b, 2 - c) if turned else (a, b, c)
                frames = slice(i + first, i + first + 2)
                window = [cols[n, h, k, frames, pl.ds(2 * core + j, 2)].reshape(128, 128) for h in range(2)]
                left.append(jnp.concatenate(window, 0))
                right.append(jnp.concatenate([kh[kernel_at, at_tap], kl[kernel_at, at_tap]], 0 if turned else 1))
            left = jnp.concatenate(left, 1)
            right = jnp.concatenate(right, 1 if turned else 0)
            product = lax.dot_general(left, right, (((1,), (1 if turned else 0,)), ((), ())), preferred_element_type=F32)
            if g == 0:
                acc[...] = product
            else:
                acc[...] += product
            yield

    def convolved():
        total = acc[0:128, 0:128] + (acc[0:128, 128:256] + acc[128:256, 0:128]) + acc[128:256, 128:256]
        return total.reshape(2, 2, 32, 128)

    def near_columns(field, n, frames):
        def one(j, _):
            columns(field, n, 2 * core + j, frames)
            return 0

        lax.fori_loop(0, 4, one, 0)

    own_of, other_of = (range(2, 6), range(0, 4)), (range(0, 2), range(4, 6))
    early, late = (2, 0), (0, 2)

    for copy in beside + near:
        copy.wait_recv()
    for n, into in ((0, pre), (1, d_active)):
        near_columns(ext, n, own_of[n])
        for _ in convolve(n, n, n == 1, early[n]):
            pass
        into[early[n] : early[n] + 2] = convolved()
    for copies in far:
        for copy in copies:
            copy.wait_recv()
    halo_frames, own_frames = pl.ds(4 * core, 2), pl.ds(2 - 2 * core, 4)
    outer_rows = pl.ds(4 * core, 2)
    passed = [
        put(ext.at[core, halo_frames, outer_rows], ext.at[core, halo_frames, outer_rows], partner),
        put(ext.at[core, own_frames, 5 * core], ext.at[core, own_frames, 5 * core], partner),
    ]

    for n, into in ((0, pre), (1, d_active)):
        near_columns(ext, n, other_of[n])
        for _ in convolve(n, n, n == 1, late[n]):
            pass
        into[late[n] : late[n] + 2] = convolved()
    v = pre[...]
    s = jax.nn.sigmoid(v)
    ext2[0, 2:6, own] = v * s
    ext2[1, 0:4, own] = d_active[...] * s * (1.0 + v * (1.0 - s))
    swap = to_partner(ext2)

    for copy in passed:
        copy.wait_recv()

    @pl.when(core == 0)
    def _():
        for row in (4, 5):
            columns(ext, 1, row, range(6))

    @pl.when(core == 1)
    def _():
        for row in (0, 1):
            columns(ext, 0, row, range(6))

    for copy in swap:
        copy.wait_recv()
    whole = ext2[core, own_frames, 1:5].reshape(512, 128)
    fixed[0:128], fixed[128:256] = split(whole.T)

    def gradient(tap):
        a, b, c = (core * t + (1 - core) * (2 - t) for t in tap)
        right = [cols[1 - core, h, c, pl.ds(a, 4), pl.ds(b, 4)].reshape(512, 128) for h in range(2)]
        m = jnp.dot(fixed[...], jnp.concatenate(right, 1), preferred_element_type=F32)
        m = m[0:128, 0:128] + (m[0:128, 128:256] + m[128:256, 0:128]) + m[128:256, 128:256]
        part[tap_index(tap)] = jnp.where(core == 1, m.T, m).reshape(16, 8, 128)

    def stream(which, first, count, x_first):
        taps = pl.ds(first, count)
        rings = [[at(x + d, y, z) for d in (1, 2, 3)], [at(x, y + d, z) for d in (1, 2, 3)]]
        p, s = (x, y) if x_first else (y, x)
        ring, ring2 = rings if x_first else rings[::-1]
        p_of, s_of = ([lax.rem(i + d, 4) for d in range(4)] for i in (p, s))
        tile = 4 * p + s
        mine = sums.at[core]
        place = [lax.rem(z + d + 64 - first, 8) for d in range(8)]
        owns = [k < count for k in place]
        tap_at = [first + lax.rem(k, count) for k in place]
        z_of = [lax.rem(z + d, 8) for d in range(8)]

        def same(ref, to):
            return put(ref, ref, to)

        for tap in TAPS[first : first + count]:
            gradient(tap)
        yield
        sent = [put(part.at[taps, pl.ds(4 * p_of[d], 4)], r1.at[d - 1, taps], ring[d - 1]) for d in (1, 2, 3)]
        yield
        for copy in sent:
            copy.wait_recv()
        part[taps, pl.ds(4 * p, 4)] += r1[0, taps] + r1[1, taps] + r1[2, taps]
        sent = [put(part.at[taps, 4 * p + s_of[d]], r2.at[d - 1, taps], ring2[d - 1]) for d in (1, 2, 3)]
        yield
        for copy in sent:
            copy.wait_recv()
        part[taps, tile] += r2[0, taps] + r2[1, taps] + r2[2, taps]
        sent = []
        for d in range(1, 8):
            sent.append(put(part.at[tap_at[d], tile], rz.at[which, d - 1], at(x, y, z_of[d]), owns[d]))
        yield

        @pl.when(owns[0])
        def _():
            total = part[tap_at[0], tile]
            for d in range(1, 8):
                sent[d - 1].wait_recv()
                total = total + rz[which, d - 1]
            mine[tap_at[0], tile] = total * Q

        done = mine.at[tap_at[0], tile]
        sent = [put(done, done, at(x, y, z_of[d]), owns[0]) for d in range(1, 8)]
        yield
        for d in range(1, 8):
            pl.when(owns[8 - d])(sent[d - 1].wait_recv)
        sent = [same(mine.at[taps, tile], to) for to in ring2]
        yield
        for copy in sent:
            copy.wait_recv()
        sent = [same(mine.at[taps, pl.ds(4 * p, 4)], to) for to in ring]
        across = [same(mine.at[taps, pl.ds(4 * p, 4)], partner)]
        yield
        for d in (1, 2, 3):
            sent[d - 1].wait_recv()
            across.append(same(mine.at[taps, pl.ds(4 * p_of[4 - d], 4)], partner))
        yield
        for copy in across:
            copy.wait_recv()

    def stream_z(which, first, count):
        taps = pl.ds(first, count)
        got = pl.ds((which - 8) * count, count)
        z_of = [lax.rem(z + d, 8) for d in range(8)]
        mine = sums.at[core]

        def owned(xx, yy):
            o = lax.rem(lax.rem(xx, 4) + 4 * lax.rem(yy, 4) + 64 - 6 * (which - 8), 16)
            return o < 2 * count, first + lax.rem(lax.div(o, 2), count), 2 * z + lax.rem(o, 2)

        for tap in TAPS[first : first + count]:
            gradient(tap)
        yield
        sent = [put(part.at[taps, pl.ds(2 * z_of[d], 2)], c1.at[d - 1, got], at(x, y, z_of[d])) for d in range(1, 8)]
        yield
        total = part[taps, pl.ds(2 * z, 2)]
        for d in range(1, 8):
            sent[d - 1].wait_recv()
            total = total + c1[d - 1, got]
        part[taps, pl.ds(2 * z, 2)] = total
        sent = []
        for n, (dx, dy) in enumerate(plane):
            owns, tap, tile = owned(x + dx, y + dy)
            sent.append(put(part.at[tap, tile], c2.at[which - 8, n], at(x + dx, y + dy, z), owns))
        yield
        owns, tap, tile = owned(x, y)

        @pl.when(owns)
        def _():
            total = part[tap, tile]
            for n in range(15):
                sent[n].wait_recv()
                total = total + c2[which - 8, n]
            mine[tap, tile] = total * Q

        done = mine.at[tap, tile]
        sent = [put(done, done, at(x + dx, y + dy, z), owns) for dx, dy in plane]
        yield
        for n, (dx, dy) in enumerate(plane):
            pl.when(owned(x + 4 - dx, y + 4 - dy)[0])(sent[n].wait_recv)
        done = mine.at[taps, pl.ds(2 * z, 2)]
        sent = [put(done, done, at(x, y, z_of[d])) for d in range(1, 8)]
        across = [put(done, done, partner)]
        yield
        for d in range(1, 8):
            sent[d - 1].wait_recv()
            done = mine.at[taps, pl.ds(2 * z_of[8 - d], 2)]
            across.append(put(done, done, partner))
        yield
        for copy in across:
            copy.wait_recv()

    def finish():
        for n, out in ((0, block_ref), (1, gclip_ref)):
            near2, far2 = halo2
            near2[n].wait_recv()
            near_columns(ext2, n, own_of[n])
            yield
            for half in (early[n], late[n]):
                yield from convolve(n, 1 - n, n == 1, half)
                shown = half + 2 * (1 - n)
                out[half : half + 2] = ext[n, shown : shown + 2, own] + convolved()
                yield
                if half == early[n]:
                    for copy in far2[n]:
                        copy.wait_recv()
                    near_columns(ext2, n, other_of[n])
                    yield

    running, order = [], []
    for n, (first, count, axis, times) in enumerate(STREAMS):
        running.append(stream_z(n, first, count) if axis == "z" else stream(n, first, count, axis == "x"))
        order += [(time, n) for time in times]
    finishing = finish()
    halo2 = []
    order.sort()
    for at_event, (time, n) in enumerate(order):
        if time > 9.0 and not halo2:
            halo2 += to_others(ext2)
        next(running[n], None)
        if time > 14.0 and at_event + 1 < len(order):
            for _ in range(int((order[at_event + 1][0] - time) / 0.25)):
                next(finishing, None)
    for _ in finishing:
        pass
    for copy, sends in started:
        if sends is None:
            copy.wait_send()
        else:
            pl.when(sends)(copy.wait_send)


def copy_out(block_ref, gclip_ref, sums, block_out, gclip_out, one_out, two_out, sem):
    copies = []
    pieces = [(block_ref, block_out), (gclip_ref, gclip_out)]
    for n, out in ((1, one_out), (0, two_out)):
        pieces += [(sums.at[n, pl.ds(9 * i, 9)], out.at[pl.ds(9 * i, 9)]) for i in range(3)]
    for src, dst in pieces:
        copies.append(pltpu.make_async_copy(src, dst, sem.at[len(copies)]))
        copies[-1].start()
    for copy in copies:
        copy.wait()


def per_device(clip, kernel_one, kernel_two, cotangent):
    vmem = pl.BlockSpec(memory_space=pltpu.VMEM)
    hbm = pl.BlockSpec(memory_space=pltpu.HBM)
    anywhere = pl.BlockSpec(memory_space=pl.ANY)
    field = jax.ShapeDtypeStruct(clip.shape, F32)
    block_out, grad_clip, sums = pl.pallas_call(
        kernel,
        out_shape=(field, field, jax.ShapeDtypeStruct((2, 27, 16, 8, 128), F32)),
        in_specs=[hbm] * 4,
        out_specs=(vmem, vmem, vmem),
        scratch_shapes=[
            pltpu.VMEM((2, 27, 128, 128), F32),
            pltpu.VMEM((2, 27, 128, 128), BF16),
            pltpu.VMEM((2, 27, 128, 128), BF16),
            pltpu.VMEM((2, 6, 6, 32, 128), F32),
            pltpu.VMEM((2, 6, 6, 32, 128), F32),
            pltpu.VMEM((2, 2, 3, 6, 6, 32, 128), BF16),
            pltpu.VMEM((256, 256), F32),
            pltpu.VMEM((4, 2, 32, 128), F32),
            pltpu.VMEM((4, 2, 32, 128), F32),
            pltpu.VMEM((256, 512), BF16),
            pltpu.VMEM((27, 16, 8, 128), F32),
            pltpu.VMEM((3, 27, 4, 8, 128), F32),
            pltpu.VMEM((3, 27, 8, 128), F32),
            pltpu.VMEM((8, 7, 8, 128), F32),
            pltpu.VMEM((7, 6, 2, 8, 128), F32),
            pltpu.VMEM((2, 15, 8, 128), F32),
            pltpu.SemaphoreType.DMA((COPIES,)),
            pltpu.SemaphoreType.DMA((COPIES,)),
            pltpu.SemaphoreType.DMA((4,)),
        ],
        compiler_params=pltpu.CompilerParams(
            collective_id=0, has_side_effects=True, vmem_limit_bytes=32 * 1024 * 1024
        ),
        cost_estimate=pl.CostEstimate(flops=6 * 4 * 226492416, bytes_accessed=8 * 1024 * 1024, transcendentals=32768),
    )(*(pltpu.with_memory_space_constraint(a, pltpu.HBM) for a in (clip, cotangent, kernel_one.reshape(27, 128, 128), kernel_two.reshape(27, 128, 128))))
    grad = jax.ShapeDtypeStruct((27, 16, 8, 128), F32)
    block_out, grad_clip, grad_one, grad_two = pl.pallas_call(
        copy_out,
        out_shape=(field, field, grad, grad),
        in_specs=[anywhere] * 3,
        out_specs=(hbm,) * 4,
        scratch_shapes=[pltpu.SemaphoreType.DMA((8,))],
        compiler_params=pltpu.CompilerParams(vmem_limit_bytes=1024 * 1024),
        cost_estimate=pl.CostEstimate(flops=0, bytes_accessed=8 * 1024 * 1024, transcendentals=0),
    )(block_out, grad_clip, sums)
    return block_out, grad_clip, grad_one.reshape(kernel_one.shape), grad_two.reshape(kernel_two.shape)


def solution(mesh):
    field = P("tm", "rows", None, None)
    return jax.shard_map(
        per_device,
        mesh=mesh,
        in_specs=(field, P(), P(), field),
        out_specs=(field, field, P(), P()),
        check_vma=False,
    )
```

```python
import jax
import jax.numpy as jnp
from jax import lax
from jax.experimental import pallas as pl
from jax.experimental.pallas import tpu as pltpu
from jax.sharding import PartitionSpec as P

MESH = pl.DeviceIdType.MESH
F32 = jnp.float32
BF16 = jnp.bfloat16
TAPS = [(a, b, c) for a in range(3) for b in range(3) for c in range(3)]
GROUPS = [TAPS[0:8], TAPS[8:16], TAPS[16:24], TAPS[24:27]]
STREAMS = []
PAIRS = ((3, 3), (3, 3), (3, 3), (2, 2))
BEGIN = (0.1, 0.3, 0.5, 5.7)
ALONG_Z = (5,)


def plan():
    first, sent = 0, 0
    for k, counts in enumerate(PAIRS):
        sent += counts[0]
        arrive = 3.6 + 0.6 * sent
        late = [arrive + t for t in (0.0, 3.8, 8.8, 13.8, 17.6, 20.8 + 0.6 * counts[0], 99.0)]
        for n, count in enumerate(counts):
            STREAMS.append((k * 2 + n, first, count, "xy"[n], [0.05 * n + t for t in [0.2 * k, BEGIN[k]] + late]))
            first += count
    sent = 0
    for k, count in enumerate(ALONG_Z):
        begin, sent = 0.35 + 0.25 * k, sent + count
        STREAMS.append((k, first, count, "z", [begin + t for t in (0.0, 0.1, 4.6 + 1.1 * sent, 9.6 + 1.1 * sent, 14.6 + 1.1 * sent, 19.2 + 2.2 * sent, 99.5)]))
        first += count


plan()
SEMAPHORES = (22, 64)
Q = 1.0 / 256.0


def tap_index(tap):
    return (tap[0] * 3 + tap[1]) * 3 + tap[2]


def split(v):
    hi = v.astype(BF16)
    return hi, (v - hi.astype(F32)).astype(BF16)


def kernel(
    clip_ref, cot_ref, k1_ref, k2_ref,
    block_ref, gclip_ref, sums,
    kf, kh, kl, ext, ext2, cols, acc, pre, d_active, fixed, part, r1, r2, rz, c1, c2,
    send_sem, recv_sem, load_sem,
):
    tm = lax.axis_index("tm")
    rows = lax.axis_index("rows")
    x, z = lax.rem(tm, 4), lax.div(tm, 4)
    core, y = lax.rem(rows, 2), lax.div(rows, 2)

    def at(xx, yy, zz):
        return (zz * 4 + lax.rem(xx, 4), lax.rem(yy, 4) * 2 + core)

    partner_row = y * 2 + 1 - core
    outer_row = lax.rem(rows + 2 * core - 1 + 8, 8)
    tm_next, tm_prev = lax.rem(tm + 1, 32), lax.rem(tm + 31, 32)
    partner = (tm, partner_row)
    own = pl.ds(1 + 2 * core, 2)

    loads = []
    for src, dst in ((clip_ref, ext.at[0, 2:6, own]), (cot_ref, ext.at[1, 0:4, own]), (k1_ref, kf.at[0]), (k2_ref, kf.at[1])):
        loads.append(pltpu.make_async_copy(src, dst, load_sem.at[len(loads)]))
        loads[-1].start()

    peers = [partner, (tm, outer_row)]
    for t in (tm_next, tm_prev):
        peers += [(t, rows), (t, partner_row), (t, outer_row)]
    plane = [(d % 4, d // 4) for d in range(1, 16)]
    peers += [at(x + dx, y + dy, z) for dx, dy in plane]
    peers += [at(x, y, lax.rem(z + d, 8)) for d in range(1, 8)]
    barrier = pltpu.get_barrier_semaphore()
    for peer in peers:
        pl.semaphore_signal(barrier, inc=1, device_id=peer, device_id_type=MESH)
    for load in loads[:2]:
        load.wait()
    pl.semaphore_wait(barrier, len(peers))

    taken = [0, 0]

    def new(side):
        taken[side] += 1
        return taken[side] - 1

    def group():
        return new(0), new(1)

    def copy_of(src, dst, device, sems):
        return pltpu.make_async_remote_copy(
            src_ref=src, dst_ref=dst, send_sem=send_sem.at[sems[0]], recv_sem=recv_sem.at[sems[1]],
            device_id=device, device_id_type=MESH,
        )

    def put(src, dst, device, sems, sends=None):
        copy = copy_of(src, dst, device, sems)
        if sends is None:
            copy.start()
        else:
            pl.when(sends)(copy.start)

    def arrived(ref, sems):
        copy_of(ref, ref, partner, sems).wait_recv()

    def left(ref, sems):
        copy_of(ref, ref, partner, sems).wait_send()

    to_leave = []

    edge, edge_there, inner = 1 + 3 * core, 5 - 5 * core, 2 + core
    sides = ((0, pl.ds(2, 4), pl.ds(4, 2), pl.ds(0, 2), tm_next), (1, pl.ds(0, 4), pl.ds(0, 2), pl.ds(4, 2), tm_prev))

    def to_partner(field):
        sems = group()
        for n, mine, _, _, _ in sides:
            put(field.at[n, mine, own], field.at[n, mine, own], partner, sems)
        to_leave.append((field.at[:, 0:4, 0:2], sems))
        return to_leave[-1]

    def to_others(field):
        near, far = [], []
        for n, mine, _, _, _ in sides:
            near.append((field.at[n, 0:4, 0], group()))
            put(field.at[n, mine, edge], field.at[n, mine, edge_there], (tm, outer_row), near[n][1])
        for n, _, src, dst, there in sides:
            sems = group()
            put(field.at[n, src, edge], field.at[n, dst, edge_there], (there, outer_row), sems)
            put(field.at[n, src, inner], field.at[n, dst, inner], (there, partner_row), sems)
            put(field.at[n, src, own], field.at[n, dst, own], (there, rows), sems)
            far.append((field.at[n, 0:2, 0:4], sems))
        to_leave.extend(near + far)
        return near, far

    beside = to_partner(ext)
    near, far = to_others(ext)

    for load in loads[2:]:
        load.wait()

    def split_tap(t, _):
        for n in range(2):
            kh[n, t], kl[n, t] = split(kf[n, t])
        return 0

    lax.fori_loop(0, 27, split_tap, 0)
    at_column = lax.broadcasted_iota(jnp.int32, (32, 128), 0)

    def columns(field, n, row, frames):
        inside = jnp.logical_not(((row == 0) & (y == 0)) | ((row == 5) & (y == 3)))
        for f in frames:
            keep = inside
            if n == 0 and f < 2:
                keep = keep & (tm > 0)
            if n == 1 and f > 3:
                keep = keep & (tm < 31)
            v = jnp.where(keep, field[n, f, row], 0.0)
            hi = v.astype(BF16).astype(F32)
            lo = v - hi
            for h, piece in enumerate((hi, lo)):
                cols[n, h, 0, f, row] = jnp.where(at_column == 0, 0.0, pltpu.roll(piece, 1, 0)).astype(BF16)
                cols[n, h, 1, f, row] = piece.astype(BF16)
                cols[n, h, 2, f, row] = jnp.where(at_column == 31, 0.0, pltpu.roll(piece, 31, 0)).astype(BF16)

    def convolve(n, kernel_at, turned, first):
        for g, group in enumerate(GROUPS):
            left, right = [], []
            for a, b, c in group:
                at_tap = tap_index((a, b, c))
                i, j, k = (2 - a, 2 - b, 2 - c) if turned else (a, b, c)
                frames = slice(i + first, i + first + 2)
                window = [cols[n, h, k, frames, pl.ds(2 * core + j, 2)].reshape(128, 128) for h in range(2)]
                left.append(jnp.concatenate(window, 0))
                right.append(jnp.concatenate([kh[kernel_at, at_tap], kl[kernel_at, at_tap]], 0 if turned else 1))
            left = jnp.concatenate(left, 1)
            right = jnp.concatenate(right, 1 if turned else 0)
            product = lax.dot_general(left, right, (((1,), (1 if turned else 0,)), ((), ())), preferred_element_type=F32)
            if g == 0:
                acc[...] = product
            else:
                acc[...] += product
            yield

    def convolved():
        total = acc[0:128, 0:128] + (acc[0:128, 128:256] + acc[128:256, 0:128]) + acc[128:256, 128:256]
        return total.reshape(2, 2, 32, 128)

    def near_columns(field, n, frames):
        def one(j, _):
            columns(field, n, 2 * core + j, frames)
            return 0

        lax.fori_loop(0, 4, one, 0)

    own_of, other_of = (range(2, 6), range(0, 4)), (range(0, 2), range(4, 6))
    early, late = (2, 0), (0, 2)

    for copies in [beside] + near:
        arrived(*copies)
    for n, into in ((0, pre), (1, d_active)):
        near_columns(ext, n, own_of[n])
        for _ in convolve(n, n, n == 1, early[n]):
            pass
        into[early[n] : early[n] + 2] = convolved()
    for copies in far:
        arrived(*copies)
    halo_frames, own_frames = pl.ds(4 * core, 2), pl.ds(2 - 2 * core, 4)
    outer_rows = pl.ds(4 * core, 2)
    passed = (ext.at[0, 0:4, 0:2], group())
    for mine in (ext.at[core, halo_frames, outer_rows], ext.at[core, own_frames, 5 * core]):
        put(mine, mine, partner, passed[1])
    to_leave.append(passed)

    for n, into in ((0, pre), (1, d_active)):
        near_columns(ext, n, other_of[n])
        for _ in convolve(n, n, n == 1, late[n]):
            pass
        into[late[n] : late[n] + 2] = convolved()
    v = pre[...]
    s = jax.nn.sigmoid(v)
    ext2[0, 2:6, own] = v * s
    ext2[1, 0:4, own] = d_active[...] * s * (1.0 + v * (1.0 - s))
    swap = to_partner(ext2)

    arrived(*passed)

    @pl.when(core == 0)
    def _():
        for row in (4, 5):
            columns(ext, 1, row, range(6))

    @pl.when(core == 1)
    def _():
        for row in (0, 1):
            columns(ext, 0, row, range(6))

    arrived(*swap)
    whole = ext2[core, own_frames, 1:5].reshape(512, 128)
    fixed[0:128], fixed[128:256] = split(whole.T)

    def gradient(tap):
        a, b, c = (core * t + (1 - core) * (2 - t) for t in tap)
        right = [cols[1 - core, h, c, pl.ds(a, 4), pl.ds(b, 4)].reshape(512, 128) for h in range(2)]
        m = jnp.dot(fixed[...], jnp.concatenate(right, 1), preferred_element_type=F32)
        m = m[0:128, 0:128] + (m[0:128, 128:256] + m[128:256, 0:128]) + m[128:256, 128:256]
        part[tap_index(tap)] = jnp.where(core == 1, m.T, m).reshape(16, 8, 128)

    ring_sends, ring2_sends, z_sends, back_z, back_ring2, back_ring, across_sends = (new(0) for _ in range(7))
    across = (across_sends, new(1))

    def same(ref, to, sems):
        put(ref, ref, to, sems)

    def stream(which, first, count, x_first):
        taps = pl.ds(first, count)
        rings = [[at(x + d, y, z) for d in (1, 2, 3)], [at(x, y + d, z) for d in (1, 2, 3)]]
        p, s = (x, y) if x_first else (y, x)
        ring, ring2 = rings if x_first else rings[::-1]
        p_of, s_of = ([lax.rem(i + d, 4) for d in range(4)] for i in (p, s))
        tile = 4 * p + s
        mine = sums.at[core]
        place = [lax.rem(z + d + 64 - first, 8) for d in range(8)]
        owns = [k < count for k in place]
        tap_at = [first + lax.rem(k, count) for k in place]
        z_of = [lax.rem(z + d, 8) for d in range(8)]

        for tap in TAPS[first : first + count]:
            gradient(tap)
        yield
        sems = (ring_sends, new(1))
        for d in (1, 2, 3):
            put(part.at[taps, pl.ds(4 * p_of[d], 4)], r1.at[d - 1, taps], ring[d - 1], sems)
        yield
        arrived(r1.at[:, taps], sems)
        part[taps, pl.ds(4 * p, 4)] += r1[0, taps] + r1[1, taps] + r1[2, taps]
        sems = (ring2_sends, new(1))
        for d in (1, 2, 3):
            put(part.at[taps, 4 * p + s_of[d]], r2.at[d - 1, taps], ring2[d - 1], sems)
        yield
        arrived(r2.at[:, taps], sems)
        part[taps, tile] += r2[0, taps] + r2[1, taps] + r2[2, taps]
        sems = (z_sends, new(1))
        for d in range(1, 8):
            put(part.at[tap_at[d], tile], rz.at[which, d - 1], at(x, y, z_of[d]), sems, owns[d])
        yield

        @pl.when(owns[0])
        def _():
            arrived(rz.at[which], sems)
            total = part[tap_at[0], tile]
            for d in range(1, 8):
                total = total + rz[which, d - 1]
            mine[tap_at[0], tile] = total * Q

        done = mine.at[tap_at[0], tile]
        sems = (back_z, new(1))
        for d in range(1, 8):
            put(done, done, at(x, y, z_of[d]), sems, owns[0])
        yield

        @pl.when(owns[0])
        def _():
            arrived(mine.at[pl.ds(first, count - 1), tile], sems)

        @pl.when(jnp.logical_not(owns[0]))
        def _():
            arrived(mine.at[taps, tile], sems)

        sems = (back_ring2, new(1))
        for to in ring2:
            same(mine.at[taps, tile], to, sems)
        yield
        arrived(r2.at[:, taps], sems)
        sems = (back_ring, new(1))
        chunks = [mine.at[taps, pl.ds(4 * i, 4)] for i in p_of]
        for to in ring:
            same(chunks[0], to, sems)
        same(chunks[0], partner, across)
        yield
        arrived(r1.at[:, taps], sems)
        for chunk in chunks[1:]:
            same(chunk, partner, across)
        yield

    def streams_left():
        count = sum(sum(pair) for pair in PAIRS)
        each, more = divmod(count, 8)
        left(r1.at[:, 0:count], (ring_sends, 0))
        left(r1.at[:, 0:count], (back_ring, 0))
        left(r2.at[:, 0:count], (ring2_sends, 0))
        left(r2.at[:, 0:count], (back_ring2, 0))
        for some, held in ((z < more, each + 1), (z >= more, each)):

            @pl.when(some)
            def _():
                left(part.at[0 : count - held, 0], (z_sends, 0))
                left(part.at[0 : 7 * held, 0], (back_z, 0))

    def stream_z(which, first, count):
        taps = pl.ds(first, count)
        got = pl.ds(first - 27 + sum(ALONG_Z), count)
        z_of = [lax.rem(z + d, 8) for d in range(8)]
        mine = sums.at[core]

        def owned(xx, yy):
            o = lax.rem(lax.rem(xx, 4) + 4 * lax.rem(yy, 4) + 64 - 6 * which, 16)
            return o < 2 * count, first + lax.rem(lax.div(o, 2), count), 2 * z + lax.rem(o, 2)

        def when_owned(one, other):
            pl.when(owns)(one)
            pl.when(jnp.logical_not(owns))(other)

        for tap in TAPS[first : first + count]:
            gradient(tap)
        yield
        sems = group()
        to_leave.append((c1.at[:, got], sems))
        for d in range(1, 8):
            put(part.at[taps, pl.ds(2 * z_of[d], 2)], c1.at[d - 1, got], at(x, y, z_of[d]), sems)
        yield
        arrived(c1.at[:, got], sems)
        total = part[taps, pl.ds(2 * z, 2)]
        for d in range(1, 8):
            total = total + c1[d - 1, got]
        part[taps, pl.ds(2 * z, 2)] = total
        first_sems = group()
        for n, (dx, dy) in enumerate(plane):
            owns, tap, tile = owned(x + dx, y + dy)
            put(part.at[tap, tile], c2.at[which, n], at(x + dx, y + dy, z), first_sems, owns)
        yield
        owns, tap, tile = owned(x, y)

        @pl.when(owns)
        def _():
            arrived(c2.at[which], first_sems)
            total = part[tap, tile]
            for n in range(15):
                total = total + c2[which, n]
            mine[tap, tile] = total * Q

        done = mine.at[tap, tile]
        second_sems = group()
        for dx, dy in plane:
            put(done, done, at(x + dx, y + dy, z), second_sems, owns)
        yield
        fewer, all_tiles = (part.at[0 : 2 * count - n, 0] for n in (1, 0))
        when_owned(lambda: arrived(fewer, second_sems), lambda: arrived(all_tiles, second_sems))
        done = mine.at[taps, pl.ds(2 * z, 2)]
        sems = group()
        to_leave.append((c1.at[:, got], sems))
        for d in range(1, 8):
            same(done, at(x, y, z_of[d]), sems)
        same(done, partner, across)
        yield
        arrived(c1.at[:, got], sems)
        for d in range(1, 8):
            same(mine.at[taps, pl.ds(2 * z_of[d], 2)], partner, across)
        yield
        when_owned(lambda: left(fewer, first_sems), lambda: left(all_tiles, first_sems))
        pl.when(owns)(lambda: left(c2.at[which], second_sems))

    def finish():
        for n, out in ((0, block_ref), (1, gclip_ref)):
            near2, far2 = halo2
            arrived(*near2[n])
            near_columns(ext2, n, own_of[n])
            yield
            for half in (early[n], late[n]):
                yield from convolve(n, 1 - n, n == 1, half)
                shown = half + 2 * (1 - n)
                out[half : half + 2] = ext[n, shown : shown + 2, own] + convolved()
                yield
                if half == early[n]:
                    arrived(*far2[n])
                    near_columns(ext2, n, other_of[n])
                    yield

    running, order = [], []
    for n, (which, first, count, axis, times) in enumerate(STREAMS):
        running.append(stream_z(which, first, count) if axis == "z" else stream(which, first, count, axis == "x"))
        order += [(time, n) for time in times]
    finishing = finish()
    halo2 = []
    order.sort()
    for at_event, (time, n) in enumerate(order):
        if time > 9.0 and not halo2:
            halo2 += to_others(ext2)
        next(running[n], None)
        if time > 14.0 and at_event + 1 < len(order):
            for _ in range(int((order[at_event + 1][0] - time) / 0.25)):
                next(finishing, None)
    for _ in finishing:
        pass
    arrived(sums.at[1 - core], across)
    left(sums.at[core], across)
    streams_left()
    for ref, sems in to_leave:
        left(ref, sems)


def copy_out(block_ref, gclip_ref, sums, block_out, gclip_out, one_out, two_out, sem):
    copies = []
    pieces = [(block_ref, block_out), (gclip_ref, gclip_out)]
    for n, out in ((1, one_out), (0, two_out)):
        pieces += [(sums.at[n, pl.ds(9 * i, 9)], out.at[pl.ds(9 * i, 9)]) for i in range(3)]
    for src, dst in pieces:
        copies.append(pltpu.make_async_copy(src, dst, sem.at[len(copies)]))
        copies[-1].start()
    for copy in copies:
        copy.wait()


def per_device(clip, kernel_one, kernel_two, cotangent):
    vmem = pl.BlockSpec(memory_space=pltpu.VMEM)
    hbm = pl.BlockSpec(memory_space=pltpu.HBM)
    anywhere = pl.BlockSpec(memory_space=pl.ANY)
    field = jax.ShapeDtypeStruct(clip.shape, F32)
    block_out, grad_clip, sums = pl.pallas_call(
        kernel,
        out_shape=(field, field, jax.ShapeDtypeStruct((2, 27, 16, 8, 128), F32)),
        in_specs=[hbm] * 4,
        out_specs=(vmem, vmem, vmem),
        scratch_shapes=[
            pltpu.VMEM((2, 27, 128, 128), F32),
            pltpu.VMEM((2, 27, 128, 128), BF16),
            pltpu.VMEM((2, 27, 128, 128), BF16),
            pltpu.VMEM((2, 6, 6, 32, 128), F32),
            pltpu.VMEM((2, 6, 6, 32, 128), F32),
            pltpu.VMEM((2, 2, 3, 6, 6, 32, 128), BF16),
            pltpu.VMEM((256, 256), F32),
            pltpu.VMEM((4, 2, 32, 128), F32),
            pltpu.VMEM((4, 2, 32, 128), F32),
            pltpu.VMEM((256, 512), BF16),
            pltpu.VMEM((27, 16, 8, 128), F32),
            pltpu.VMEM((3, 27, 4, 8, 128), F32),
            pltpu.VMEM((3, 27, 8, 128), F32),
            pltpu.VMEM((2 * len(PAIRS), 7, 8, 128), F32),
            pltpu.VMEM((7, sum(ALONG_Z) + 1, 2, 8, 128), F32),
            pltpu.VMEM((len(ALONG_Z) + 1, 15, 8, 128), F32),
            pltpu.SemaphoreType.DMA((SEMAPHORES[0],)),
            pltpu.SemaphoreType.DMA((SEMAPHORES[1],)),
            pltpu.SemaphoreType.DMA((4,)),
        ],
        compiler_params=pltpu.CompilerParams(
            collective_id=0, has_side_effects=True, vmem_limit_bytes=32 * 1024 * 1024
        ),
        cost_estimate=pl.CostEstimate(flops=6 * 4 * 226492416, bytes_accessed=8 * 1024 * 1024, transcendentals=32768),
    )(*(pltpu.with_memory_space_constraint(a, pltpu.HBM) for a in (clip, cotangent, kernel_one.reshape(27, 128, 128), kernel_two.reshape(27, 128, 128))))
    grad = jax.ShapeDtypeStruct((27, 16, 8, 128), F32)
    block_out, grad_clip, grad_one, grad_two = pl.pallas_call(
        copy_out,
        out_shape=(field, field, grad, grad),
        in_specs=[anywhere] * 3,
        out_specs=(hbm,) * 4,
        scratch_shapes=[pltpu.SemaphoreType.DMA((8,))],
        compiler_params=pltpu.CompilerParams(vmem_limit_bytes=1024 * 1024),
        cost_estimate=pl.CostEstimate(flops=0, bytes_accessed=8 * 1024 * 1024, transcendentals=0),
    )(block_out, grad_clip, sums)
    return block_out, grad_clip, grad_one.reshape(kernel_one.shape), grad_two.reshape(kernel_two.shape)


def solution(mesh):
    field = P("tm", "rows", None, None)
    return jax.shard_map(
        per_device,
        mesh=mesh,
        in_specs=(field, P(), P(), field),
        out_specs=(field, field, P(), P()),
        check_vma=False,
    )
```

```python
import jax
import jax.numpy as jnp
from jax import lax
from jax.experimental import pallas as pl
from jax.experimental.pallas import tpu as pltpu
from jax.sharding import PartitionSpec as P

MESH = pl.DeviceIdType.MESH
F32 = jnp.float32
BF16 = jnp.bfloat16
TAPS = [(a, b, c) for a in range(3) for b in range(3) for c in range(3)]
GROUPS = [TAPS[0:8], TAPS[8:16], TAPS[16:24], TAPS[24:27]]
STREAMS = []
PAIRS = ((3, 3), (3, 3), (3, 3), (2, 2))
BEGIN = (0.1, 0.3, 0.5, 5.7)
ALONG_Z = (5,)


def plan():
    first, sent = 0, 0
    for k, counts in enumerate(PAIRS):
        sent += counts[0]
        arrive = 3.6 + 0.6 * sent
        late = [arrive + t for t in (0.0, 3.8, 8.8, 13.8, 17.6, 20.8 + 0.6 * counts[0], 99.0)]
        for n, count in enumerate(counts):
            STREAMS.append((k * 2 + n, first, count, "xy"[n], [0.05 * n + t for t in [0.2 * k, BEGIN[k]] + late]))
            first += count
    sent = 0
    for k, count in enumerate(ALONG_Z):
        begin, sent = 0.35 + 0.25 * k, sent + count
        STREAMS.append((k, first, count, "z", [begin + t for t in (0.0, 0.1, 4.6 + 1.1 * sent, 9.6 + 1.1 * sent, 14.6 + 1.1 * sent, 19.2 + 2.2 * sent, 99.5)]))
        first += count


plan()
SEMAPHORES = (23, 65)
Q = 1.0 / 256.0


def tap_index(tap):
    return (tap[0] * 3 + tap[1]) * 3 + tap[2]


def split(v):
    hi = v.astype(BF16)
    return hi, (v - hi.astype(F32)).astype(BF16)


def kernel(
    clip_ref, cot_ref, k1_ref, k2_ref,
    block_ref, gclip_ref, sums,
    kf, kh, kl, ext, ext2, cols, acc, pre, d_active, fixed, part, r1, r2, rz, c1, c2,
    send_sem, recv_sem, load_sem,
):
    tm = lax.axis_index("tm")
    rows = lax.axis_index("rows")
    x, z = lax.rem(tm, 4), lax.div(tm, 4)
    core, y = lax.rem(rows, 2), lax.div(rows, 2)

    def at(xx, yy, zz):
        return (zz * 4 + lax.rem(xx, 4), lax.rem(yy, 4) * 2 + core)

    partner_row = y * 2 + 1 - core
    outer_row = lax.rem(rows + 2 * core - 1 + 8, 8)
    tm_next, tm_prev = lax.rem(tm + 1, 32), lax.rem(tm + 31, 32)
    partner = (tm, partner_row)
    own = pl.ds(1 + 2 * core, 2)

    loads = []
    for src, dst in ((clip_ref, ext.at[0, 2:6, own]), (cot_ref, ext.at[1, 0:4, own]), (k1_ref, kf.at[0]), (k2_ref, kf.at[1])):
        loads.append(pltpu.make_async_copy(src, dst, load_sem.at[len(loads)]))
        loads[-1].start()

    peers = [partner, (tm, outer_row)]
    for t in (tm_next, tm_prev):
        peers += [(t, rows), (t, partner_row), (t, outer_row)]
    plane = [(d % 4, d // 4) for d in range(1, 16)]
    peers += [at(x + dx, y + dy, z) for dx, dy in plane]
    peers += [at(x, y, lax.rem(z + d, 8)) for d in range(1, 8)]
    barrier = pltpu.get_barrier_semaphore()
    for peer in peers:
        pl.semaphore_signal(barrier, inc=1, device_id=peer, device_id_type=MESH)
    pl.semaphore_wait(barrier, len(peers))

    taken = [0, 0]

    def new(side):
        taken[side] += 1
        return taken[side] - 1

    def group():
        return new(0), new(1)

    def copy_of(src, dst, device, sems):
        return pltpu.make_async_remote_copy(
            src_ref=src, dst_ref=dst, send_sem=send_sem.at[sems[0]], recv_sem=recv_sem.at[sems[1]],
            device_id=device, device_id_type=MESH,
        )

    def put(src, dst, device, sems, sends=None):
        copy = copy_of(src, dst, device, sems)
        if sends is None:
            copy.start()
        else:
            pl.when(sends)(copy.start)

    def arrived(ref, sems):
        copy_of(ref, ref, partner, sems).wait_recv()

    def left(ref, sems):
        copy_of(ref, ref, partner, sems).wait_send()

    to_leave = []

    edge, edge_there, inner = 1 + 3 * core, 5 - 5 * core, 2 + core
    sides = ((0, pl.ds(2, 4), pl.ds(4, 2), pl.ds(0, 2), tm_next), (1, pl.ds(0, 4), pl.ds(0, 2), pl.ds(4, 2), tm_prev))

    def to_others(field, seen):
        near, far = [], []
        for n, mine, _, _, _ in sides:
            near.append((field.at[n, 0:4, 0], group()))
            put(seen(n, mine, edge), field.at[n, mine, edge_there], (tm, outer_row), near[n][1])
        for n, _, src, dst, there in sides:
            sems = group()
            put(seen(n, src, edge), field.at[n, dst, edge_there], (there, outer_row), sems)
            put(seen(n, src, inner), field.at[n, dst, inner], (there, partner_row), sems)
            put(seen(n, src, own), field.at[n, dst, own], (there, rows), sems)
            far.append((field.at[n, 0:2, 0:4], sems))
        to_leave.extend(near + far)
        return near, far

    def operand(n, frames, at_rows):
        ref = (clip_ref, cot_ref)[n]
        frames = pl.ds(frames.start - 2 * (1 - n), frames.size)
        if at_rows is own:
            return ref.at[frames]
        return ref.at[frames, core if at_rows is edge else 1 - core]

    near, far = to_others(ext, operand)
    beside = (ext.at[:, 0:4, 0:2], group())
    for n, mine, _, _, _ in sides:
        put(operand(n, mine, own), ext.at[n, mine, own], partner, beside[1])
    to_leave.append(beside)

    for load in loads[:2]:
        load.wait()
    for load in loads[2:]:
        load.wait()

    def split_tap(t, _):
        for n in range(2):
            kh[n, t], kl[n, t] = split(kf[n, t])
        return 0

    lax.fori_loop(0, 27, split_tap, 0)
    at_column = lax.broadcasted_iota(jnp.int32, (32, 128), 0)

    def columns(field, n, row, frames):
        inside = jnp.logical_not(((row == 0) & (y == 0)) | ((row == 5) & (y == 3)))
        for f in frames:
            keep = inside
            if n == 0 and f < 2:
                keep = keep & (tm > 0)
            if n == 1 and f > 3:
                keep = keep & (tm < 31)
            v = jnp.where(keep, field[n, f, row], 0.0)
            hi = v.astype(BF16).astype(F32)
            lo = v - hi
            for h, piece in enumerate((hi, lo)):
                cols[n, h, 0, f, row] = jnp.where(at_column == 0, 0.0, pltpu.roll(piece, 1, 0)).astype(BF16)
                cols[n, h, 1, f, row] = piece.astype(BF16)
                cols[n, h, 2, f, row] = jnp.where(at_column == 31, 0.0, pltpu.roll(piece, 31, 0)).astype(BF16)

    def convolve(n, kernel_at, turned, first, slot=0, groups=GROUPS, more=False):
        for group_taps in groups:
            lhs, rhs = [], []
            for a, b, c in group_taps:
                at_tap = tap_index((a, b, c))
                i, j, k = (2 - a, 2 - b, 2 - c) if turned else (a, b, c)
                frames = slice(i + first, i + first + 2)
                window = [cols[n, h, k, frames, pl.ds(2 * core + j, 2)].reshape(128, 128) for h in range(2)]
                lhs.append(jnp.concatenate(window, 0))
                rhs.append(jnp.concatenate([kh[kernel_at, at_tap], kl[kernel_at, at_tap]], 0 if turned else 1))
            lhs = jnp.concatenate(lhs, 1)
            rhs = jnp.concatenate(rhs, 1 if turned else 0)
            product = lax.dot_general(lhs, rhs, (((1,), (1 if turned else 0,)), ((), ())), preferred_element_type=F32)
            if more:
                acc[slot] += product
            else:
                acc[slot] = product
            more = True
            yield

    def convolved(slot=0):
        total = acc[slot, 0:128, 0:128] + (acc[slot, 0:128, 128:256] + acc[slot, 128:256, 0:128]) + acc[slot, 128:256, 128:256]
        return total.reshape(2, 2, 32, 128)

    def near_columns(field, n, frames):
        def one(j, _):
            columns(field, n, 2 * core + j, frames)
            return 0

        lax.fori_loop(0, 4, one, 0)

    own_of, other_of = (range(2, 6), range(0, 4)), (range(0, 2), range(4, 6))
    early, late = (2, 0), (0, 2)

    for copies in [beside] + near:
        arrived(*copies)
    for n, into in ((0, pre), (1, d_active)):
        near_columns(ext, n, own_of[n])
        for _ in convolve(n, n, n == 1, early[n]):
            pass
        into[early[n] : early[n] + 2] = convolved()
    for n in range(2):
        for _ in convolve(n, n, n == 1, late[n], 1 + n, [TAPS[18:26], TAPS[26:27]]):
            pass
    for copies in far:
        arrived(*copies)
    halo_frames, own_frames = pl.ds(4 * core, 2), pl.ds(2 - 2 * core, 4)
    outer_rows = pl.ds(4 * core, 2)
    passed = (ext.at[0, 0:4, 0:2], group())
    for mine in (ext.at[core, halo_frames, outer_rows], ext.at[core, own_frames, 5 * core]):
        put(mine, mine, partner, passed[1])
    to_leave.append(passed)

    for n, into in ((0, pre), (1, d_active)):
        near_columns(ext, n, other_of[n])
        for _ in convolve(n, n, n == 1, late[n], 1 + n, [TAPS[0:8], TAPS[8:16], TAPS[16:18]], True):
            pass
        into[late[n] : late[n] + 2] = convolved(1 + n)
    v = pre[...]
    s = jax.nn.sigmoid(v)
    ext2[0, 2:6, own] = v * s
    ext2[1, 0:4, own] = d_active[...] * s * (1.0 + v * (1.0 - s))
    swap, swap2 = ((ext2.at[0, 0:4, 0:2], group()) for _ in range(2))
    for n, frames, copies in ((1 - core, pl.ds(2 * core, 4), swap), (core, pl.ds(2 - 2 * core, 4), swap2)):
        put(ext2.at[n, frames, own], ext2.at[n, frames, own], partner, copies[1])
    to_leave += [swap, swap2]

    arrived(*passed)

    @pl.when(core == 0)
    def _():
        for row in (4, 5):
            columns(ext, 1, row, range(6))

    @pl.when(core == 1)
    def _():
        for row in (0, 1):
            columns(ext, 0, row, range(6))

    arrived(*swap)
    whole = ext2[core, own_frames, 1:5].reshape(512, 128)
    fixed[0:128], fixed[128:256] = split(whole.T)

    def gradient(tap):
        a, b, c = (core * t + (1 - core) * (2 - t) for t in tap)
        right = [cols[1 - core, h, c, pl.ds(a, 4), pl.ds(b, 4)].reshape(512, 128) for h in range(2)]
        m = jnp.dot(fixed[...], jnp.concatenate(right, 1), preferred_element_type=F32)
        m = m[0:128, 0:128] + (m[0:128, 128:256] + m[128:256, 0:128]) + m[128:256, 128:256]
        part[tap_index(tap)] = jnp.where(core == 1, m.T, m).reshape(16, 8, 128)

    ring_sends, ring2_sends, z_sends, back_z, back_ring2, back_ring, across_sends = (new(0) for _ in range(7))
    across = (across_sends, new(1))

    def same(ref, to, sems):
        put(ref, ref, to, sems)

    def stream(which, first, count, x_first):
        taps = pl.ds(first, count)
        rings = [[at(x + d, y, z) for d in (1, 2, 3)], [at(x, y + d, z) for d in (1, 2, 3)]]
        p, s = (x, y) if x_first else (y, x)
        ring, ring2 = rings if x_first else rings[::-1]
        p_of, s_of = ([lax.rem(i + d, 4) for d in range(4)] for i in (p, s))
        tile = 4 * p + s
        mine = sums.at[core]
        place = [lax.rem(z + d + 64 - first, 8) for d in range(8)]
        owns = [k < count for k in place]
        tap_at = [first + lax.rem(k, count) for k in place]
        z_of = [lax.rem(z + d, 8) for d in range(8)]

        for tap in TAPS[first : first + count]:
            gradient(tap)
        yield
        sems = (ring_sends, new(1))
        for d in (1, 2, 3):
            put(part.at[taps, pl.ds(4 * p_of[d], 4)], r1.at[d - 1, taps], ring[d - 1], sems)
        yield
        arrived(r1.at[:, taps], sems)
        part[taps, pl.ds(4 * p, 4)] += r1[0, taps] + r1[1, taps] + r1[2, taps]
        sems = (ring2_sends, new(1))
        for d in (1, 2, 3):
            put(part.at[taps, 4 * p + s_of[d]], r2.at[d - 1, taps], ring2[d - 1], sems)
        yield
        arrived(r2.at[:, taps], sems)
        part[taps, tile] += r2[0, taps] + r2[1, taps] + r2[2, taps]
        sems = (z_sends, new(1))
        for d in range(1, 8):
            put(part.at[tap_at[d], tile], rz.at[which, d - 1], at(x, y, z_of[d]), sems, owns[d])
        yield

        @pl.when(owns[0])
        def _():
            arrived(rz.at[which], sems)
            total = part[tap_at[0], tile]
            for d in range(1, 8):
                total = total + rz[which, d - 1]
            mine[tap_at[0], tile] = total * Q

        done = mine.at[tap_at[0], tile]
        sems = (back_z, new(1))
        for d in range(1, 8):
            put(done, done, at(x, y, z_of[d]), sems, owns[0])
        yield

        @pl.when(owns[0])
        def _():
            arrived(mine.at[pl.ds(first, count - 1), tile], sems)

        @pl.when(jnp.logical_not(owns[0]))
        def _():
            arrived(mine.at[taps, tile], sems)

        sems = (back_ring2, new(1))
        for to in ring2:
            same(mine.at[taps, tile], to, sems)
        yield
        arrived(r2.at[:, taps], sems)
        sems = (back_ring, new(1))
        chunks = [mine.at[taps, pl.ds(4 * i, 4)] for i in p_of]
        for to in ring:
            same(chunks[0], to, sems)
        same(chunks[0], partner, across)
        yield
        arrived(r1.at[:, taps], sems)
        for chunk in chunks[1:]:
            same(chunk, partner, across)
        yield

    def streams_left():
        count = sum(sum(pair) for pair in PAIRS)
        each, more = divmod(count, 8)
        left(r1.at[:, 0:count], (ring_sends, 0))
        left(r1.at[:, 0:count], (back_ring, 0))
        left(r2.at[:, 0:count], (ring2_sends, 0))
        left(r2.at[:, 0:count], (back_ring2, 0))
        for some, held in ((z < more, each + 1), (z >= more, each)):

            @pl.when(some)
            def _():
                left(part.at[0 : count - held, 0], (z_sends, 0))
                left(part.at[0 : 7 * held, 0], (back_z, 0))

    def stream_z(which, first, count):
        taps = pl.ds(first, count)
        got = pl.ds(first - 27 + sum(ALONG_Z), count)
        z_of = [lax.rem(z + d, 8) for d in range(8)]
        mine = sums.at[core]

        def owned(xx, yy):
            o = lax.rem(lax.rem(xx, 4) + 4 * lax.rem(yy, 4) + 64 - 6 * which, 16)
            return o < 2 * count, first + lax.rem(lax.div(o, 2), count), 2 * z + lax.rem(o, 2)

        def when_owned(one, other):
            pl.when(owns)(one)
            pl.when(jnp.logical_not(owns))(other)

        for tap in TAPS[first : first + count]:
            gradient(tap)
        yield
        sems = group()
        to_leave.append((c1.at[:, got], sems))
        for d in range(1, 8):
            put(part.at[taps, pl.ds(2 * z_of[d], 2)], c1.at[d - 1, got], at(x, y, z_of[d]), sems)
        yield
        arrived(c1.at[:, got], sems)
        total = part[taps, pl.ds(2 * z, 2)]
        for d in range(1, 8):
            total = total + c1[d - 1, got]
        part[taps, pl.ds(2 * z, 2)] = total
        first_sems = group()
        for n, (dx, dy) in enumerate(plane):
            owns, tap, tile = owned(x + dx, y + dy)
            put(part.at[tap, tile], c2.at[which, n], at(x + dx, y + dy, z), first_sems, owns)
        yield
        owns, tap, tile = owned(x, y)

        @pl.when(owns)
        def _():
            arrived(c2.at[which], first_sems)
            total = part[tap, tile]
            for n in range(15):
                total = total + c2[which, n]
            mine[tap, tile] = total * Q

        done = mine.at[tap, tile]
        second_sems = group()
        for dx, dy in plane:
            put(done, done, at(x + dx, y + dy, z), second_sems, owns)
        yield
        fewer, all_tiles = (part.at[0 : 2 * count - n, 0] for n in (1, 0))
        when_owned(lambda: arrived(fewer, second_sems), lambda: arrived(all_tiles, second_sems))
        done = mine.at[taps, pl.ds(2 * z, 2)]
        sems = group()
        to_leave.append((c1.at[:, got], sems))
        for d in range(1, 8):
            same(done, at(x, y, z_of[d]), sems)
        same(done, partner, across)
        yield
        arrived(c1.at[:, got], sems)
        for d in range(1, 8):
            same(mine.at[taps, pl.ds(2 * z_of[d], 2)], partner, across)
        yield
        when_owned(lambda: left(fewer, first_sems), lambda: left(all_tiles, first_sems))
        pl.when(owns)(lambda: left(c2.at[which], second_sems))

    def finish():
        for n, out in ((0, block_ref), (1, gclip_ref)):
            near2, far2 = halo2
            if n == 0:
                arrived(*swap2)
            arrived(*near2[n])
            near_columns(ext2, n, own_of[n])
            yield
            for half in (early[n], late[n]):
                yield from convolve(n, 1 - n, n == 1, half)
                shown = half + 2 * (1 - n)
                out[half : half + 2] = ext[n, shown : shown + 2, own] + convolved()
                yield
                if half == early[n]:
                    arrived(*far2[n])
                    near_columns(ext2, n, other_of[n])
                    yield

    running, order = [], []
    for n, (which, first, count, axis, times) in enumerate(STREAMS):
        running.append(stream_z(which, first, count) if axis == "z" else stream(which, first, count, axis == "x"))
        order += [(time, n) for time in times]
    finishing = finish()
    halo2 = []
    order.sort()
    for at_event, (time, n) in enumerate(order):
        if time > 9.0 and not halo2:
            halo2 += to_others(ext2, lambda n, frames, at_rows: ext2.at[n, frames, at_rows])
        next(running[n], None)
        if time > 14.0 and at_event + 1 < len(order):
            for _ in range(int((order[at_event + 1][0] - time) / 0.25)):
                next(finishing, None)
    for _ in finishing:
        pass
    arrived(sums.at[1 - core], across)
    left(sums.at[core], across)
    streams_left()
    for ref, sems in to_leave:
        left(ref, sems)


def copy_out(block_ref, gclip_ref, sums, block_out, gclip_out, one_out, two_out, sem):
    copies = []
    pieces = [(block_ref, block_out), (gclip_ref, gclip_out)]
    for n, out in ((1, one_out), (0, two_out)):
        pieces += [(sums.at[n, pl.ds(9 * i, 9)], out.at[pl.ds(9 * i, 9)]) for i in range(3)]
    for src, dst in pieces:
        copies.append(pltpu.make_async_copy(src, dst, sem.at[len(copies)]))
        copies[-1].start()
    for copy in copies:
        copy.wait()


def per_device(clip, kernel_one, kernel_two, cotangent):
    vmem = pl.BlockSpec(memory_space=pltpu.VMEM)
    hbm = pl.BlockSpec(memory_space=pltpu.HBM)
    anywhere = pl.BlockSpec(memory_space=pl.ANY)
    field = jax.ShapeDtypeStruct(clip.shape, F32)
    block_out, grad_clip, sums = pl.pallas_call(
        kernel,
        out_shape=(field, field, jax.ShapeDtypeStruct((2, 27, 16, 8, 128), F32)),
        in_specs=[hbm] * 4,
        out_specs=(vmem, vmem, vmem),
        scratch_shapes=[
            pltpu.VMEM((2, 27, 128, 128), F32),
            pltpu.VMEM((2, 27, 128, 128), BF16),
            pltpu.VMEM((2, 27, 128, 128), BF16),
            pltpu.VMEM((2, 6, 6, 32, 128), F32),
            pltpu.VMEM((2, 6, 6, 32, 128), F32),
            pltpu.VMEM((2, 2, 3, 6, 6, 32, 128), BF16),
            pltpu.VMEM((3, 256, 256), F32),
            pltpu.VMEM((4, 2, 32, 128), F32),
            pltpu.VMEM((4, 2, 32, 128), F32),
            pltpu.VMEM((256, 512), BF16),
            pltpu.VMEM((27, 16, 8, 128), F32),
            pltpu.VMEM((3, 27, 4, 8, 128), F32),
            pltpu.VMEM((3, 27, 8, 128), F32),
            pltpu.VMEM((2 * len(PAIRS), 7, 8, 128), F32),
            pltpu.VMEM((7, sum(ALONG_Z) + 1, 2, 8, 128), F32),
            pltpu.VMEM((len(ALONG_Z) + 1, 15, 8, 128), F32),
            pltpu.SemaphoreType.DMA((SEMAPHORES[0],)),
            pltpu.SemaphoreType.DMA((SEMAPHORES[1],)),
            pltpu.SemaphoreType.DMA((4,)),
        ],
        compiler_params=pltpu.CompilerParams(
            collective_id=0, has_side_effects=True, vmem_limit_bytes=32 * 1024 * 1024
        ),
        cost_estimate=pl.CostEstimate(flops=6 * 4 * 226492416, bytes_accessed=8 * 1024 * 1024, transcendentals=32768),
    )(*(pltpu.with_memory_space_constraint(a, pltpu.HBM) for a in (clip, cotangent, kernel_one.reshape(27, 128, 128), kernel_two.reshape(27, 128, 128))))
    grad = jax.ShapeDtypeStruct((27, 16, 8, 128), F32)
    block_out, grad_clip, grad_one, grad_two = pl.pallas_call(
        copy_out,
        out_shape=(field, field, grad, grad),
        in_specs=[anywhere] * 3,
        out_specs=(hbm,) * 4,
        scratch_shapes=[pltpu.SemaphoreType.DMA((8,))],
        compiler_params=pltpu.CompilerParams(vmem_limit_bytes=1024 * 1024),
        cost_estimate=pl.CostEstimate(flops=0, bytes_accessed=8 * 1024 * 1024, transcendentals=0),
    )(block_out, grad_clip, sums)
    return block_out, grad_clip, grad_one.reshape(kernel_one.shape), grad_two.reshape(kernel_two.shape)


def solution(mesh):
    field = P("tm", "rows", None, None)
    return jax.shard_map(
        per_device,
        mesh=mesh,
        in_specs=(field, P(), P(), field),
        out_specs=(field, field, P(), P()),
        check_vma=False,
    )
```

```python
import jax
import jax.numpy as jnp
from jax import lax
from jax.experimental import pallas as pl
from jax.experimental.pallas import tpu as pltpu
from jax.sharding import PartitionSpec as P

MESH = pl.DeviceIdType.MESH
F32 = jnp.float32
BF16 = jnp.bfloat16
TAPS = [(a, b, c) for a in range(3) for b in range(3) for c in range(3)]
GROUPS = [TAPS[0:8], TAPS[8:16], TAPS[16:24], TAPS[24:27]]
STREAMS = []
PAIRS = ((3, 3), (3, 3), (3, 3), (2, 2))
BEGIN = (0.1, 0.3, 0.5, 5.7)
ALONG_Z = (5,)


def plan():
    first, sent = 0, 0
    for k, counts in enumerate(PAIRS):
        sent += counts[0]
        arrive = 3.6 + 0.6 * sent
        late = [arrive + t for t in (0.0, 3.8, 8.8, 13.8, 17.6, 20.8 + 0.6 * counts[0], 99.0)]
        for n, count in enumerate(counts):
            STREAMS.append((k * 2 + n, first, count, "xy"[n], [0.05 * n + t for t in [0.2 * k, BEGIN[k]] + late]))
            first += count
    sent = 0
    for k, count in enumerate(ALONG_Z):
        begin, sent = 0.35 + 0.25 * k, sent + count
        STREAMS.append((k, first, count, "z", [begin + t for t in (0.0, 0.1, 4.6 + 1.1 * sent, 9.6 + 1.1 * sent, 14.6 + 1.1 * sent, 19.2 + 2.2 * sent, 99.5)]))
        first += count


plan()
SEMAPHORES = (23, 65)
FAR_FIRST = (4, 3, 5, 2, 6, 1, 7)
Q = 1.0 / 256.0


def tap_index(tap):
    return (tap[0] * 3 + tap[1]) * 3 + tap[2]


def split(v):
    hi = v.astype(BF16)
    return hi, (v - hi.astype(F32)).astype(BF16)


def kernel(
    clip_ref, cot_ref, k1_ref, k2_ref,
    block_ref, gclip_ref, sums,
    kf, kh, kl, ext, ext2, cols, acc, pre, d_active, fixed, part, r1, r2, rz, c1, c2,
    send_sem, recv_sem, load_sem,
):
    tm = lax.axis_index("tm")
    rows = lax.axis_index("rows")
    x, z = lax.rem(tm, 4), lax.div(tm, 4)
    core, y = lax.rem(rows, 2), lax.div(rows, 2)

    def at(xx, yy, zz):
        return (zz * 4 + lax.rem(xx, 4), lax.rem(yy, 4) * 2 + core)

    partner_row = y * 2 + 1 - core
    outer_row = lax.rem(rows + 2 * core - 1 + 8, 8)
    tm_next, tm_prev = lax.rem(tm + 1, 32), lax.rem(tm + 31, 32)
    partner = (tm, partner_row)
    own = pl.ds(1 + 2 * core, 2)

    loads = []
    for src, dst in ((clip_ref, ext.at[0, 2:6, own]), (cot_ref, ext.at[1, 0:4, own]), (k1_ref, kf.at[0]), (k2_ref, kf.at[1])):
        loads.append(pltpu.make_async_copy(src, dst, load_sem.at[len(loads)]))
        loads[-1].start()

    plane = sorted(((d % 4, d // 4) for d in range(1, 16)), key=lambda to: -sum(min(d, 4 - d) for d in to))
    peers = [at(x, y, lax.rem(z + d, 8)) for d in FAR_FIRST]
    peers += [at(x + dx, y + dy, z) for dx, dy in plane]
    for t in (tm_next, tm_prev):
        peers += [(t, outer_row), (t, partner_row), (t, rows)]
    peers += [(tm, outer_row), partner]
    barrier = pltpu.get_barrier_semaphore()
    for peer in peers:
        pl.semaphore_signal(barrier, inc=1, device_id=peer, device_id_type=MESH)
    pl.semaphore_wait(barrier, len(peers))

    taken = [0, 0]

    def new(side):
        taken[side] += 1
        return taken[side] - 1

    def group():
        return new(0), new(1)

    def copy_of(src, dst, device, sems):
        return pltpu.make_async_remote_copy(
            src_ref=src, dst_ref=dst, send_sem=send_sem.at[sems[0]], recv_sem=recv_sem.at[sems[1]],
            device_id=device, device_id_type=MESH,
        )

    def put(src, dst, device, sems, sends=None):
        copy = copy_of(src, dst, device, sems)
        if sends is None:
            copy.start()
        else:
            pl.when(sends)(copy.start)

    def arrived(ref, sems):
        copy_of(ref, ref, partner, sems).wait_recv()

    def left(ref, sems):
        copy_of(ref, ref, partner, sems).wait_send()

    to_leave = []

    edge, edge_there, inner = 1 + 3 * core, 5 - 5 * core, 2 + core
    sides = ((0, pl.ds(2, 4), pl.ds(4, 2), pl.ds(0, 2), tm_next), (1, pl.ds(0, 4), pl.ds(0, 2), pl.ds(4, 2), tm_prev))

    def to_others(field, seen):
        near, far = [], []
        for n, mine, _, _, _ in sides:
            near.append((field.at[n, 0:4, 0], group()))
            put(seen(n, mine, edge), field.at[n, mine, edge_there], (tm, outer_row), near[n][1])
        for n, _, src, dst, there in sides:
            sems = group()
            put(seen(n, src, edge), field.at[n, dst, edge_there], (there, outer_row), sems)
            put(seen(n, src, inner), field.at[n, dst, inner], (there, partner_row), sems)
            put(seen(n, src, own), field.at[n, dst, own], (there, rows), sems)
            far.append((field.at[n, 0:2, 0:4], sems))
        to_leave.extend(near + far)
        return near, far

    def operand(n, frames, at_rows):
        ref = (clip_ref, cot_ref)[n]
        frames = pl.ds(frames.start - 2 * (1 - n), frames.size)
        if at_rows is own:
            return ref.at[frames]
        return ref.at[frames, core if at_rows is edge else 1 - core]

    beside = (ext.at[:, 0:4, 0:2], group())
    for n, mine, _, _, _ in sides:
        put(operand(n, mine, own), ext.at[n, mine, own], partner, beside[1])
    to_leave.append(beside)

    near, far = to_others(ext, operand)
    for load in loads[:2]:
        load.wait()
    for load in loads[2:]:
        load.wait()

    def split_tap(t, _):
        for n in range(2):
            kh[n, t], kl[n, t] = split(kf[n, t])
        return 0

    lax.fori_loop(0, 27, split_tap, 0)
    at_column = lax.broadcasted_iota(jnp.int32, (32, 128), 0)

    def columns(field, n, row, frames):
        inside = jnp.logical_not(((row == 0) & (y == 0)) | ((row == 5) & (y == 3)))
        for f in frames:
            keep = inside
            if n == 0 and f < 2:
                keep = keep & (tm > 0)
            if n == 1 and f > 3:
                keep = keep & (tm < 31)
            v = jnp.where(keep, field[n, f, row], 0.0)
            hi = v.astype(BF16).astype(F32)
            lo = v - hi
            for h, piece in enumerate((hi, lo)):
                cols[n, h, 0, f, row] = jnp.where(at_column == 0, 0.0, pltpu.roll(piece, 1, 0)).astype(BF16)
                cols[n, h, 1, f, row] = piece.astype(BF16)
                cols[n, h, 2, f, row] = jnp.where(at_column == 31, 0.0, pltpu.roll(piece, 31, 0)).astype(BF16)

    def convolve(n, kernel_at, turned, first, slot=0, groups=GROUPS, more=False):
        for group_taps in groups:
            lhs, rhs = [], []
            for a, b, c in group_taps:
                at_tap = tap_index((a, b, c))
                i, j, k = (2 - a, 2 - b, 2 - c) if turned else (a, b, c)
                frames = slice(i + first, i + first + 2)
                window = [cols[n, h, k, frames, pl.ds(2 * core + j, 2)].reshape(128, 128) for h in range(2)]
                lhs.append(jnp.concatenate(window, 0))
                rhs.append(jnp.concatenate([kh[kernel_at, at_tap], kl[kernel_at, at_tap]], 0 if turned else 1))
            lhs = jnp.concatenate(lhs, 1)
            rhs = jnp.concatenate(rhs, 1 if turned else 0)
            product = lax.dot_general(lhs, rhs, (((1,), (1 if turned else 0,)), ((), ())), preferred_element_type=F32)
            if more:
                acc[slot] += product
            else:
                acc[slot] = product
            more = True
            yield

    def convolved(slot=0):
        total = acc[slot, 0:128, 0:128] + (acc[slot, 0:128, 128:256] + acc[slot, 128:256, 0:128]) + acc[slot, 128:256, 128:256]
        return total.reshape(2, 2, 32, 128)

    def near_columns(field, n, frames):
        def one(j, _):
            columns(field, n, 2 * core + j, frames)
            return 0

        lax.fori_loop(0, 4, one, 0)

    own_of, other_of = (range(2, 6), range(0, 4)), (range(0, 2), range(4, 6))
    early, late = (2, 0), (0, 2)

    for copies in [beside] + near:
        arrived(*copies)
    for n, into in ((0, pre), (1, d_active)):
        near_columns(ext, n, own_of[n])
        for _ in convolve(n, n, n == 1, early[n]):
            pass
        into[early[n] : early[n] + 2] = convolved()
    for n in range(2):
        for _ in convolve(n, n, n == 1, late[n], 1 + n, [TAPS[18:26], TAPS[26:27]]):
            pass
    for copies in far:
        arrived(*copies)
    halo_frames, own_frames = pl.ds(4 * core, 2), pl.ds(2 - 2 * core, 4)
    outer_rows = pl.ds(4 * core, 2)
    passed = (ext.at[0, 0:4, 0:2], group())
    for mine in (ext.at[core, halo_frames, outer_rows], ext.at[core, own_frames, 5 * core]):
        put(mine, mine, partner, passed[1])
    to_leave.append(passed)

    for n, into in ((0, pre), (1, d_active)):
        near_columns(ext, n, other_of[n])
        for _ in convolve(n, n, n == 1, late[n], 1 + n, [TAPS[0:8], TAPS[8:16], TAPS[16:18]], True):
            pass
        into[late[n] : late[n] + 2] = convolved(1 + n)
    v = pre[...]
    s = jax.nn.sigmoid(v)
    ext2[0, 2:6, own] = v * s
    ext2[1, 0:4, own] = d_active[...] * s * (1.0 + v * (1.0 - s))
    swap, swap2 = ((ext2.at[0, 0:4, 0:2], group()) for _ in range(2))
    for n, frames, copies in ((1 - core, pl.ds(2 * core, 4), swap), (core, pl.ds(2 - 2 * core, 4), swap2)):
        put(ext2.at[n, frames, own], ext2.at[n, frames, own], partner, copies[1])
    to_leave += [swap, swap2]

    arrived(*passed)

    @pl.when(core == 0)
    def _():
        for row in (4, 5):
            columns(ext, 1, row, range(6))

    @pl.when(core == 1)
    def _():
        for row in (0, 1):
            columns(ext, 0, row, range(6))

    arrived(*swap)
    whole = ext2[core, own_frames, 1:5].reshape(512, 128)
    fixed[0:128], fixed[128:256] = split(whole.T)

    def gradient(tap):
        a, b, c = (core * t + (1 - core) * (2 - t) for t in tap)
        right = [cols[1 - core, h, c, pl.ds(a, 4), pl.ds(b, 4)].reshape(512, 128) for h in range(2)]
        m = jnp.dot(fixed[...], jnp.concatenate(right, 1), preferred_element_type=F32)
        m = m[0:128, 0:128] + (m[0:128, 128:256] + m[128:256, 0:128]) + m[128:256, 128:256]
        part[tap_index(tap)] = jnp.where(core == 1, m.T, m).reshape(16, 8, 128)

    ring_sends, ring2_sends, z_sends, back_z, back_ring2, back_ring, across_sends = (new(0) for _ in range(7))
    across = (across_sends, new(1))

    def same(ref, to, sems):
        put(ref, ref, to, sems)

    def stream(which, first, count, x_first):
        taps = pl.ds(first, count)
        rings = [[at(x + d, y, z) for d in (1, 2, 3)], [at(x, y + d, z) for d in (1, 2, 3)]]
        p, s = (x, y) if x_first else (y, x)
        ring, ring2 = rings if x_first else rings[::-1]
        p_of, s_of = ([lax.rem(i + d, 4) for d in range(4)] for i in (p, s))
        tile = 4 * p + s
        mine = sums.at[core]
        place = [lax.rem(z + d + 64 - first, 8) for d in range(8)]
        owns = [k < count for k in place]
        tap_at = [first + lax.rem(k, count) for k in place]
        z_of = [lax.rem(z + d, 8) for d in range(8)]

        for tap in TAPS[first : first + count]:
            gradient(tap)
        yield
        sems = (ring_sends, new(1))
        for d in (2, 1, 3):
            put(part.at[taps, pl.ds(4 * p_of[d], 4)], r1.at[d - 1, taps], ring[d - 1], sems)
        yield
        arrived(r1.at[:, taps], sems)
        part[taps, pl.ds(4 * p, 4)] += r1[0, taps] + r1[1, taps] + r1[2, taps]
        sems = (ring2_sends, new(1))
        for d in (2, 1, 3):
            put(part.at[taps, 4 * p + s_of[d]], r2.at[d - 1, taps], ring2[d - 1], sems)
        yield
        arrived(r2.at[:, taps], sems)
        part[taps, tile] += r2[0, taps] + r2[1, taps] + r2[2, taps]
        sems = (z_sends, new(1))
        for d in FAR_FIRST:
            put(part.at[tap_at[d], tile], rz.at[which, d - 1], at(x, y, z_of[d]), sems, owns[d])
        yield

        @pl.when(owns[0])
        def _():
            arrived(rz.at[which], sems)
            total = part[tap_at[0], tile]
            for d in range(1, 8):
                total = total + rz[which, d - 1]
            mine[tap_at[0], tile] = total * Q

        done = mine.at[tap_at[0], tile]
        sems = (back_z, new(1))
        for d in FAR_FIRST:
            put(done, done, at(x, y, z_of[d]), sems, owns[0])
        yield

        @pl.when(owns[0])
        def _():
            arrived(mine.at[pl.ds(first, count - 1), tile], sems)

        @pl.when(jnp.logical_not(owns[0]))
        def _():
            arrived(mine.at[taps, tile], sems)

        sems = (back_ring2, new(1))
        for to in (ring2[1], ring2[0], ring2[2]):
            same(mine.at[taps, tile], to, sems)
        yield
        arrived(r2.at[:, taps], sems)
        sems = (back_ring, new(1))
        chunks = [mine.at[taps, pl.ds(4 * i, 4)] for i in p_of]
        for to in (ring[1], ring[0], ring[2]):
            same(chunks[0], to, sems)
        same(chunks[0], partner, across)
        yield
        arrived(r1.at[:, taps], sems)
        for chunk in chunks[1:]:
            same(chunk, partner, across)
        yield

    def streams_left():
        count = sum(sum(pair) for pair in PAIRS)
        each, more = divmod(count, 8)
        left(r1.at[:, 0:count], (ring_sends, 0))
        left(r1.at[:, 0:count], (back_ring, 0))
        left(r2.at[:, 0:count], (ring2_sends, 0))
        left(r2.at[:, 0:count], (back_ring2, 0))
        for some, held in ((z < more, each + 1), (z >= more, each)):

            @pl.when(some)
            def _():
                left(part.at[0 : count - held, 0], (z_sends, 0))
                left(part.at[0 : 7 * held, 0], (back_z, 0))

    def stream_z(which, first, count):
        taps = pl.ds(first, count)
        got = pl.ds(first - 27 + sum(ALONG_Z), count)
        z_of = [lax.rem(z + d, 8) for d in range(8)]
        mine = sums.at[core]

        def owned(xx, yy):
            o = lax.rem(lax.rem(xx, 4) + 4 * lax.rem(yy, 4) + 64 - 6 * which, 16)
            return o < 2 * count, first + lax.rem(lax.div(o, 2), count), 2 * z + lax.rem(o, 2)

        def when_owned(one, other):
            pl.when(owns)(one)
            pl.when(jnp.logical_not(owns))(other)

        for tap in TAPS[first : first + count]:
            gradient(tap)
        yield
        sems = group()
        to_leave.append((c1.at[:, got], sems))
        for d in FAR_FIRST:
            put(part.at[taps, pl.ds(2 * z_of[d], 2)], c1.at[d - 1, got], at(x, y, z_of[d]), sems)
        yield
        arrived(c1.at[:, got], sems)
        total = part[taps, pl.ds(2 * z, 2)]
        for d in range(1, 8):
            total = total + c1[d - 1, got]
        part[taps, pl.ds(2 * z, 2)] = total
        first_sems = group()
        for n, (dx, dy) in enumerate(plane):
            owns, tap, tile = owned(x + dx, y + dy)
            put(part.at[tap, tile], c2.at[which, n], at(x + dx, y + dy, z), first_sems, owns)
        yield
        owns, tap, tile = owned(x, y)

        @pl.when(owns)
        def _():
            arrived(c2.at[which], first_sems)
            total = part[tap, tile]
            for n in range(15):
                total = total + c2[which, n]
            mine[tap, tile] = total * Q

        done = mine.at[tap, tile]
        second_sems = group()
        for dx, dy in plane:
            put(done, done, at(x + dx, y + dy, z), second_sems, owns)
        yield
        fewer, all_tiles = (part.at[0 : 2 * count - n, 0] for n in (1, 0))
        when_owned(lambda: arrived(fewer, second_sems), lambda: arrived(all_tiles, second_sems))
        done = mine.at[taps, pl.ds(2 * z, 2)]
        sems = group()
        to_leave.append((c1.at[:, got], sems))
        for d in FAR_FIRST:
            same(done, at(x, y, z_of[d]), sems)
        same(done, partner, across)
        yield
        arrived(c1.at[:, got], sems)
        for d in range(1, 8):
            same(mine.at[taps, pl.ds(2 * z_of[d], 2)], partner, across)
        yield
        when_owned(lambda: left(fewer, first_sems), lambda: left(all_tiles, first_sems))
        pl.when(owns)(lambda: left(c2.at[which], second_sems))

    def finish():
        for n, out in ((0, block_ref), (1, gclip_ref)):
            near2, far2 = halo2
            if n == 0:
                arrived(*swap2)
            arrived(*near2[n])
            near_columns(ext2, n, own_of[n])
            yield
            for half in (early[n], late[n]):
                yield from convolve(n, 1 - n, n == 1, half)
                shown = half + 2 * (1 - n)
                out[half : half + 2] = ext[n, shown : shown + 2, own] + convolved()
                yield
                if half == early[n]:
                    arrived(*far2[n])
                    near_columns(ext2, n, other_of[n])
                    yield

    running, order = [], []
    for n, (which, first, count, axis, times) in enumerate(STREAMS):
        running.append(stream_z(which, first, count) if axis == "z" else stream(which, first, count, axis == "x"))
        order += [(time, n) for time in times]
    finishing = finish()
    halo2 = []
    order.sort()
    for at_event, (time, n) in enumerate(order):
        if time > 9.0 and not halo2:
            halo2 += to_others(ext2, lambda n, frames, at_rows: ext2.at[n, frames, at_rows])
        next(running[n], None)
        if time > 14.0 and at_event + 1 < len(order):
            for _ in range(int((order[at_event + 1][0] - time) / 0.25)):
                next(finishing, None)
    for _ in finishing:
        pass
    arrived(sums.at[1 - core], across)
    left(sums.at[core], across)
    streams_left()
    for ref, sems in to_leave:
        left(ref, sems)


def copy_out(block_ref, gclip_ref, sums, block_out, gclip_out, one_out, two_out, sem):
    copies = []
    pieces = [(block_ref, block_out), (gclip_ref, gclip_out)]
    for n, out in ((1, one_out), (0, two_out)):
        pieces += [(sums.at[n, pl.ds(9 * i, 9)], out.at[pl.ds(9 * i, 9)]) for i in range(3)]
    for src, dst in pieces:
        copies.append(pltpu.make_async_copy(src, dst, sem.at[len(copies)]))
        copies[-1].start()
    for copy in copies:
        copy.wait()


def per_device(clip, kernel_one, kernel_two, cotangent):
    vmem = pl.BlockSpec(memory_space=pltpu.VMEM)
    hbm = pl.BlockSpec(memory_space=pltpu.HBM)
    anywhere = pl.BlockSpec(memory_space=pl.ANY)
    field = jax.ShapeDtypeStruct(clip.shape, F32)
    block_out, grad_clip, sums = pl.pallas_call(
        kernel,
        out_shape=(field, field, jax.ShapeDtypeStruct((2, 27, 16, 8, 128), F32)),
        in_specs=[hbm] * 4,
        out_specs=(vmem, vmem, vmem),
        scratch_shapes=[
            pltpu.VMEM((2, 27, 128, 128), F32),
            pltpu.VMEM((2, 27, 128, 128), BF16),
            pltpu.VMEM((2, 27, 128, 128), BF16),
            pltpu.VMEM((2, 6, 6, 32, 128), F32),
            pltpu.VMEM((2, 6, 6, 32, 128), F32),
            pltpu.VMEM((2, 2, 3, 6, 6, 32, 128), BF16),
            pltpu.VMEM((3, 256, 256), F32),
            pltpu.VMEM((4, 2, 32, 128), F32),
            pltpu.VMEM((4, 2, 32, 128), F32),
            pltpu.VMEM((256, 512), BF16),
            pltpu.VMEM((27, 16, 8, 128), F32),
            pltpu.VMEM((3, 27, 4, 8, 128), F32),
            pltpu.VMEM((3, 27, 8, 128), F32),
            pltpu.VMEM((2 * len(PAIRS), 7, 8, 128), F32),
            pltpu.VMEM((7, sum(ALONG_Z) + 1, 2, 8, 128), F32),
            pltpu.VMEM((len(ALONG_Z) + 1, 15, 8, 128), F32),
            pltpu.SemaphoreType.DMA((SEMAPHORES[0],)),
            pltpu.SemaphoreType.DMA((SEMAPHORES[1],)),
            pltpu.SemaphoreType.DMA((4,)),
        ],
        compiler_params=pltpu.CompilerParams(
            collective_id=0, has_side_effects=True, vmem_limit_bytes=32 * 1024 * 1024
        ),
        cost_estimate=pl.CostEstimate(flops=6 * 4 * 226492416, bytes_accessed=8 * 1024 * 1024, transcendentals=32768),
    )(*(pltpu.with_memory_space_constraint(a, pltpu.HBM) for a in (clip, cotangent, kernel_one.reshape(27, 128, 128), kernel_two.reshape(27, 128, 128))))
    grad = jax.ShapeDtypeStruct((27, 16, 8, 128), F32)
    block_out, grad_clip, grad_one, grad_two = pl.pallas_call(
        copy_out,
        out_shape=(field, field, grad, grad),
        in_specs=[anywhere] * 3,
        out_specs=(hbm,) * 4,
        scratch_shapes=[pltpu.SemaphoreType.DMA((8,))],
        compiler_params=pltpu.CompilerParams(vmem_limit_bytes=1024 * 1024),
        cost_estimate=pl.CostEstimate(flops=0, bytes_accessed=8 * 1024 * 1024, transcendentals=0),
    )(block_out, grad_clip, sums)
    return block_out, grad_clip, grad_one.reshape(kernel_one.shape), grad_two.reshape(kernel_two.shape)


def solution(mesh):
    field = P("tm", "rows", None, None)
    return jax.shard_map(
        per_device,
        mesh=mesh,
        in_specs=(field, P(), P(), field),
        out_specs=(field, field, P(), P()),
        check_vma=False,
    )
```

```python
import jax
import jax.numpy as jnp
from jax import lax
from jax.experimental import pallas as pl
from jax.experimental.pallas import tpu as pltpu
from jax.sharding import PartitionSpec as P

MESH = pl.DeviceIdType.MESH
F32 = jnp.float32
BF16 = jnp.bfloat16
TAPS = [(a, b, c) for a in range(3) for b in range(3) for c in range(3)]
GROUPS = [TAPS[0:8], TAPS[8:16], TAPS[16:24], TAPS[24:27]]
STREAMS = []
PAIRS = ((3, 3), (3, 3), (3, 3), (2, 2))
BEGIN = (0.1, 0.3, 0.5, 5.7)
ALONG_Z = (5,)


def plan():
    first, sent = 0, 0
    for k, counts in enumerate(PAIRS):
        sent += counts[0]
        arrive = 3.6 + 0.6 * sent
        late = [arrive + t for t in (0.0, 3.8, 8.8, 13.8, 17.6, 20.8 + 0.6 * counts[0], 99.0)]
        for n, count in enumerate(counts):
            STREAMS.append((k * 2 + n, first, count, "xy"[n], [0.05 * n + t for t in [0.2 * k, BEGIN[k]] + late]))
            first += count
    sent = 0
    for k, count in enumerate(ALONG_Z):
        begin, sent = 0.35 + 0.25 * k, sent + count
        STREAMS.append((k, first, count, "z", [begin + t for t in (0.0, 0.1, 4.6 + 1.1 * sent, 9.6 + 1.1 * sent, 14.6 + 1.1 * sent, 19.2 + 2.2 * sent, 99.5)]))
        first += count


plan()
SEMAPHORES = (23, 65)
FAR_FIRST = (4, 3, 5, 2, 6, 1, 7)
Q = 1.0 / 256.0


def tap_index(tap):
    return (tap[0] * 3 + tap[1]) * 3 + tap[2]


def split(v):
    hi = v.astype(BF16)
    return hi, (v - hi.astype(F32)).astype(BF16)


def kernel(
    clip_ref, cot_ref, k1_ref, k2_ref,
    block_ref, gclip_ref, sums,
    kf, kh, kl, ext, ext2, cols, acc, pre, d_active, fixed, part, r1, r2, rz, c1, c2,
    send_sem, recv_sem, load_sem,
):
    tm = lax.axis_index("tm")
    rows = lax.axis_index("rows")
    x, z = lax.rem(tm, 4), lax.div(tm, 4)
    core, y = lax.rem(rows, 2), lax.div(rows, 2)

    def at(xx, yy, zz):
        return (zz * 4 + lax.rem(xx, 4), lax.rem(yy, 4) * 2 + core)

    partner_row = y * 2 + 1 - core
    outer_row = lax.rem(rows + 2 * core - 1 + 8, 8)
    tm_next, tm_prev = lax.rem(tm + 1, 32), lax.rem(tm + 31, 32)
    partner = (tm, partner_row)
    own = pl.ds(1 + 2 * core, 2)

    loads = []
    for src, dst in ((clip_ref, ext.at[0, 2:6, own]), (cot_ref, ext.at[1, 0:4, own]), (k1_ref, kf.at[0]), (k2_ref, kf.at[1])):
        loads.append(pltpu.make_async_copy(src, dst, load_sem.at[len(loads)]))
        loads[-1].start()

    plane = sorted(((d % 4, d // 4) for d in range(1, 16)), key=lambda to: -sum(min(d, 4 - d) for d in to))
    peers = [at(x, y, lax.rem(z + d, 8)) for d in FAR_FIRST]
    peers += [at(x + dx, y + dy, z) for dx, dy in plane]
    for t in (tm_next, tm_prev):
        peers += [(t, outer_row), (t, partner_row), (t, rows)]
    peers += [(tm, outer_row), partner]
    barrier = pltpu.get_barrier_semaphore()
    for peer in peers:
        pl.semaphore_signal(barrier, inc=1, device_id=peer, device_id_type=MESH)
    pl.semaphore_wait(barrier, len(peers))

    taken = [0, 0]

    def new(side):
        taken[side] += 1
        return taken[side] - 1

    def group():
        return new(0), new(1)

    def copy_of(src, dst, device, sems):
        return pltpu.make_async_remote_copy(
            src_ref=src, dst_ref=dst, send_sem=send_sem.at[sems[0]], recv_sem=recv_sem.at[sems[1]],
            device_id=device, device_id_type=MESH,
        )

    def put(src, dst, device, sems, sends=None):
        copy = copy_of(src, dst, device, sems)
        if sends is None:
            copy.start()
        else:
            pl.when(sends)(copy.start)

    def arrived(ref, sems):
        copy_of(ref, ref, partner, sems).wait_recv()

    def left(ref, sems):
        copy_of(ref, ref, partner, sems).wait_send()

    to_leave = []

    edge, edge_there, inner = 1 + 3 * core, 5 - 5 * core, 2 + core
    sides = ((0, pl.ds(2, 4), pl.ds(4, 2), pl.ds(0, 2), tm_next), (1, pl.ds(0, 4), pl.ds(0, 2), pl.ds(4, 2), tm_prev))

    def to_others(field, seen):
        near, far = [], []
        for n, mine, _, _, _ in sides:
            near.append((field.at[n, 0:4, 0], group()))
            put(seen(n, mine, edge), field.at[n, mine, edge_there], (tm, outer_row), near[n][1])
        for n, _, src, dst, there in sides:
            sems = group()
            put(seen(n, src, edge), field.at[n, dst, edge_there], (there, outer_row), sems)
            put(seen(n, src, inner), field.at[n, dst, inner], (there, partner_row), sems)
            put(seen(n, src, own), field.at[n, dst, own], (there, rows), sems)
            far.append((field.at[n, 0:2, 0:4], sems))
        to_leave.extend(near + far)
        return near, far

    def operand(n, frames, at_rows):
        ref = (clip_ref, cot_ref)[n]
        frames = pl.ds(frames.start - 2 * (1 - n), frames.size)
        if at_rows is own:
            return ref.at[frames]
        return ref.at[frames, core if at_rows is edge else 1 - core]

    beside = (ext.at[:, 0:4, 0:2], group())
    for n, mine, _, _, _ in sides:
        put(operand(n, mine, own), ext.at[n, mine, own], partner, beside[1])
    to_leave.append(beside)

    near, far = to_others(ext, operand)
    for load in loads[:2]:
        load.wait()
    for load in loads[2:]:
        load.wait()

    def split_tap(t, _):
        for n in range(2):
            kh[n, t], kl[n, t] = split(kf[n, t])
        return 0

    lax.fori_loop(0, 27, split_tap, 0)
    at_column = lax.broadcasted_iota(jnp.int32, (32, 128), 0)

    def columns(field, n, row, frames):
        inside = jnp.logical_not(((row == 0) & (y == 0)) | ((row == 5) & (y == 3)))
        for f in frames:
            keep = inside
            if n == 0 and f < 2:
                keep = keep & (tm > 0)
            if n == 1 and f > 3:
                keep = keep & (tm < 31)
            v = jnp.where(keep, field[n, f, row], 0.0)
            hi = v.astype(BF16).astype(F32)
            lo = v - hi
            for h, piece in enumerate((hi, lo)):
                cols[n, h, 0, f, row] = jnp.where(at_column == 0, 0.0, pltpu.roll(piece, 1, 0)).astype(BF16)
                cols[n, h, 1, f, row] = piece.astype(BF16)
                cols[n, h, 2, f, row] = jnp.where(at_column == 31, 0.0, pltpu.roll(piece, 31, 0)).astype(BF16)

    def convolve(n, kernel_at, turned, first, slot=0, groups=GROUPS, more=False):
        for group_taps in groups:
            lhs, rhs = [], []
            for a, b, c in group_taps:
                at_tap = tap_index((a, b, c))
                i, j, k = (2 - a, 2 - b, 2 - c) if turned else (a, b, c)
                frames = slice(i + first, i + first + 2)
                window = [cols[n, h, k, frames, pl.ds(2 * core + j, 2)].reshape(128, 128) for h in range(2)]
                lhs.append(jnp.concatenate(window, 0))
                rhs.append(jnp.concatenate([kh[kernel_at, at_tap], kl[kernel_at, at_tap]], 0 if turned else 1))
            lhs = jnp.concatenate(lhs, 1)
            rhs = jnp.concatenate(rhs, 1 if turned else 0)
            product = lax.dot_general(lhs, rhs, (((1,), (1 if turned else 0,)), ((), ())), preferred_element_type=F32)
            if more:
                acc[slot] += product
            else:
                acc[slot] = product
            more = True
            yield

    def convolved(slot=0):
        total = acc[slot, 0:128, 0:128] + (acc[slot, 0:128, 128:256] + acc[slot, 128:256, 0:128]) + acc[slot, 128:256, 128:256]
        return total.reshape(2, 2, 32, 128)

    def near_columns(field, n, frames):
        def one(j, _):
            columns(field, n, 2 * core + j, frames)
            return 0

        lax.fori_loop(0, 4, one, 0)

    own_of, other_of = (range(2, 6), range(0, 4)), (range(0, 2), range(4, 6))
    early, late = (2, 0), (0, 2)

    for copies in [beside] + near:
        arrived(*copies)
    for n, into in ((0, pre), (1, d_active)):
        near_columns(ext, n, own_of[n])
        for _ in convolve(n, n, n == 1, early[n]):
            pass
        into[early[n] : early[n] + 2] = convolved()
    for n in range(2):
        for _ in convolve(n, n, n == 1, late[n], 1 + n, [TAPS[18:26], TAPS[26:27]]):
            pass
    for copies in far:
        arrived(*copies)
    halo_frames, own_frames = pl.ds(4 * core, 2), pl.ds(2 - 2 * core, 4)
    outer_rows = pl.ds(4 * core, 2)
    passed = (ext.at[0, 0:4, 0:2], group())
    for mine in (ext.at[core, halo_frames, outer_rows], ext.at[core, own_frames, 5 * core]):
        put(mine, mine, partner, passed[1])
    to_leave.append(passed)

    for n, into in ((0, pre), (1, d_active)):
        near_columns(ext, n, other_of[n])
        for _ in convolve(n, n, n == 1, late[n], 1 + n, [TAPS[0:8], TAPS[8:16], TAPS[16:18]], True):
            pass
        into[late[n] : late[n] + 2] = convolved(1 + n)
    v = pre[...]
    s = jax.nn.sigmoid(v)
    ext2[0, 2:6, own] = v * s
    ext2[1, 0:4, own] = d_active[...] * s * (1.0 + v * (1.0 - s))
    swap, swap2 = ((ext2.at[0, 0:4, 0:2], group()) for _ in range(2))
    for n, frames, copies in ((1 - core, pl.ds(2 * core, 4), swap), (core, pl.ds(2 - 2 * core, 4), swap2)):
        put(ext2.at[n, frames, own], ext2.at[n, frames, own], partner, copies[1])
    to_leave += [swap, swap2]

    arrived(*passed)

    @pl.when(core == 0)
    def _():
        for row in (4, 5):
            columns(ext, 1, row, range(6))

    @pl.when(core == 1)
    def _():
        for row in (0, 1):
            columns(ext, 0, row, range(6))

    arrived(*swap)
    whole = ext2[core, own_frames, 1:5].reshape(512, 128)
    fixed[0:128], fixed[128:256] = split(whole.T)

    def gradient(tap):
        a, b, c = (core * t + (1 - core) * (2 - t) for t in tap)
        right = [cols[1 - core, h, c, pl.ds(a, 4), pl.ds(b, 4)].reshape(512, 128) for h in range(2)]
        m = jnp.dot(fixed[...], jnp.concatenate(right, 1), preferred_element_type=F32)
        m = m[0:128, 0:128] + (m[0:128, 128:256] + m[128:256, 0:128]) + m[128:256, 128:256]
        part[tap_index(tap)] = jnp.where(core == 1, m.T, m).reshape(16, 8, 128)

    ring_sends, ring2_sends, z_sends, back_z, back_ring2, back_ring, across_sends = (new(0) for _ in range(7))
    across = (across_sends, new(1))

    def same(ref, to, sems):
        put(ref, ref, to, sems)

    def stream(which, first, count, x_first):
        taps = pl.ds(first, count)
        rings = [[at(x + d, y, z) for d in (1, 2, 3)], [at(x, y + d, z) for d in (1, 2, 3)]]
        p, s = (x, y) if x_first else (y, x)
        ring, ring2 = rings if x_first else rings[::-1]
        p_of, s_of = ([lax.rem(i + d, 4) for d in range(4)] for i in (p, s))
        tile = 4 * p + s
        mine = sums.at[core]
        place = [lax.rem(z + d + 64 - first, 8) for d in range(8)]
        owns = [k < count for k in place]
        tap_at = [first + lax.rem(k, count) for k in place]
        z_of = [lax.rem(z + d, 8) for d in range(8)]

        for tap in TAPS[first : first + count]:
            gradient(tap)
        yield
        sems = (ring_sends, new(1))
        for d in (2, 1, 3):
            put(part.at[taps, pl.ds(4 * p_of[d], 4)], r1.at[d - 1, taps], ring[d - 1], sems)
        yield
        arrived(r1.at[:, taps], sems)
        part[taps, pl.ds(4 * p, 4)] += r1[0, taps] + r1[1, taps] + r1[2, taps]
        sems = (ring2_sends, new(1))
        for d in (2, 1, 3):
            put(part.at[taps, 4 * p + s_of[d]], r2.at[d - 1, taps], ring2[d - 1], sems)
        yield
        arrived(r2.at[:, taps], sems)
        part[taps, tile] += r2[0, taps] + r2[1, taps] + r2[2, taps]
        sems = (z_sends, new(1))
        for d in FAR_FIRST:
            put(part.at[tap_at[d], tile], rz.at[which, d - 1], at(x, y, z_of[d]), sems, owns[d])
        yield

        @pl.when(owns[0])
        def _():
            arrived(rz.at[which], sems)
            total = part[tap_at[0], tile]
            for d in range(1, 8):
                total = total + rz[which, d - 1]
            mine[tap_at[0], tile] = total * Q

        done = mine.at[tap_at[0], tile]
        sems = (back_z, new(1))
        for d in FAR_FIRST:
            put(done, done, at(x, y, z_of[d]), sems, owns[0])
        yield

        @pl.when(owns[0])
        def _():
            arrived(mine.at[pl.ds(first, count - 1), tile], sems)

        @pl.when(jnp.logical_not(owns[0]))
        def _():
            arrived(mine.at[taps, tile], sems)

        sems = (back_ring2, new(1))
        for to in (ring2[1], ring2[0], ring2[2]):
            same(mine.at[taps, tile], to, sems)
        yield
        arrived(r2.at[:, taps], sems)
        sems = (back_ring, new(1))
        chunks = [mine.at[taps, pl.ds(4 * i, 4)] for i in p_of]
        same(chunks[0], partner, across)
        for to in (ring[1], ring[0], ring[2]):
            same(chunks[0], to, sems)
        yield
        arrived(r1.at[:, taps], sems)
        for chunk in chunks[1:]:
            same(chunk, partner, across)
        yield

    def streams_left():
        count = sum(sum(pair) for pair in PAIRS)
        each, more = divmod(count, 8)
        left(r1.at[:, 0:count], (ring_sends, 0))
        left(r1.at[:, 0:count], (back_ring, 0))
        left(r2.at[:, 0:count], (ring2_sends, 0))
        left(r2.at[:, 0:count], (back_ring2, 0))
        for some, held in ((z < more, each + 1), (z >= more, each)):

            @pl.when(some)
            def _():
                left(part.at[0 : count - held, 0], (z_sends, 0))
                left(part.at[0 : 7 * held, 0], (back_z, 0))

    def stream_z(which, first, count):
        taps = pl.ds(first, count)
        got = pl.ds(first - 27 + sum(ALONG_Z), count)
        z_of = [lax.rem(z + d, 8) for d in range(8)]
        mine = sums.at[core]

        def owned(xx, yy):
            o = lax.rem(lax.rem(xx, 4) + 4 * lax.rem(yy, 4) + 64 - 6 * which, 16)
            return o < 2 * count, first + lax.rem(lax.div(o, 2), count), 2 * z + lax.rem(o, 2)

        def when_owned(one, other):
            pl.when(owns)(one)
            pl.when(jnp.logical_not(owns))(other)

        for tap in TAPS[first : first + count]:
            gradient(tap)
        yield
        sems = group()
        to_leave.append((c1.at[:, got], sems))
        for d in FAR_FIRST:
            put(part.at[taps, pl.ds(2 * z_of[d], 2)], c1.at[d - 1, got], at(x, y, z_of[d]), sems)
        yield
        arrived(c1.at[:, got], sems)
        total = part[taps, pl.ds(2 * z, 2)]
        for d in range(1, 8):
            total = total + c1[d - 1, got]
        part[taps, pl.ds(2 * z, 2)] = total
        first_sems = group()
        for n, (dx, dy) in enumerate(plane):
            owns, tap, tile = owned(x + dx, y + dy)
            put(part.at[tap, tile], c2.at[which, n], at(x + dx, y + dy, z), first_sems, owns)
        yield
        owns, tap, tile = owned(x, y)

        @pl.when(owns)
        def _():
            arrived(c2.at[which], first_sems)
            total = part[tap, tile]
            for n in range(15):
                total = total + c2[which, n]
            mine[tap, tile] = total * Q

        done = mine.at[tap, tile]
        second_sems = group()
        for dx, dy in plane:
            put(done, done, at(x + dx, y + dy, z), second_sems, owns)
        yield
        fewer, all_tiles = (part.at[0 : 2 * count - n, 0] for n in (1, 0))
        when_owned(lambda: arrived(fewer, second_sems), lambda: arrived(all_tiles, second_sems))
        done = mine.at[taps, pl.ds(2 * z, 2)]
        sems = group()
        to_leave.append((c1.at[:, got], sems))
        same(done, partner, across)
        for d in FAR_FIRST:
            same(done, at(x, y, z_of[d]), sems)
        yield
        arrived(c1.at[:, got], sems)
        for d in range(1, 8):
            same(mine.at[taps, pl.ds(2 * z_of[d], 2)], partner, across)
        yield
        when_owned(lambda: left(fewer, first_sems), lambda: left(all_tiles, first_sems))
        pl.when(owns)(lambda: left(c2.at[which], second_sems))

    def finish():
        for n, out in ((0, block_ref), (1, gclip_ref)):
            near2, far2 = halo2
            if n == 0:
                arrived(*swap2)
            arrived(*near2[n])
            near_columns(ext2, n, own_of[n])
            yield
            for half in (early[n], late[n]):
                yield from convolve(n, 1 - n, n == 1, half)
                shown = half + 2 * (1 - n)
                out[half : half + 2] = ext[n, shown : shown + 2, own] + convolved()
                yield
                if half == early[n]:
                    arrived(*far2[n])
                    near_columns(ext2, n, other_of[n])
                    yield

    running, order = [], []
    for n, (which, first, count, axis, times) in enumerate(STREAMS):
        running.append(stream_z(which, first, count) if axis == "z" else stream(which, first, count, axis == "x"))
        order += [(time, n) for time in times]
    finishing = finish()
    halo2 = []
    order.sort()
    for at_event, (time, n) in enumerate(order):
        if time > 9.0 and not halo2:
            halo2 += to_others(ext2, lambda n, frames, at_rows: ext2.at[n, frames, at_rows])
        next(running[n], None)
        if time > 14.0 and at_event + 1 < len(order):
            for _ in range(int((order[at_event + 1][0] - time) / 0.25)):
                next(finishing, None)
    for _ in finishing:
        pass
    arrived(sums.at[1 - core], across)
    left(sums.at[core], across)
    streams_left()
    for ref, sems in to_leave:
        left(ref, sems)


def copy_out(block_ref, gclip_ref, sums, block_out, gclip_out, one_out, two_out, sem):
    copies = []
    pieces = [(block_ref, block_out), (gclip_ref, gclip_out)]
    for n, out in ((1, one_out), (0, two_out)):
        pieces += [(sums.at[n, pl.ds(9 * i, 9)], out.at[pl.ds(9 * i, 9)]) for i in range(3)]
    for src, dst in pieces:
        copies.append(pltpu.make_async_copy(src, dst, sem.at[len(copies)]))
        copies[-1].start()
    for copy in copies:
        copy.wait()


def per_device(clip, kernel_one, kernel_two, cotangent):
    vmem = pl.BlockSpec(memory_space=pltpu.VMEM)
    hbm = pl.BlockSpec(memory_space=pltpu.HBM)
    anywhere = pl.BlockSpec(memory_space=pl.ANY)
    field = jax.ShapeDtypeStruct(clip.shape, F32)
    block_out, grad_clip, sums = pl.pallas_call(
        kernel,
        out_shape=(field, field, jax.ShapeDtypeStruct((2, 27, 16, 8, 128), F32)),
        in_specs=[hbm] * 4,
        out_specs=(vmem, vmem, vmem),
        scratch_shapes=[
            pltpu.VMEM((2, 27, 128, 128), F32),
            pltpu.VMEM((2, 27, 128, 128), BF16),
            pltpu.VMEM((2, 27, 128, 128), BF16),
            pltpu.VMEM((2, 6, 6, 32, 128), F32),
            pltpu.VMEM((2, 6, 6, 32, 128), F32),
            pltpu.VMEM((2, 2, 3, 6, 6, 32, 128), BF16),
            pltpu.VMEM((3, 256, 256), F32),
            pltpu.VMEM((4, 2, 32, 128), F32),
            pltpu.VMEM((4, 2, 32, 128), F32),
            pltpu.VMEM((256, 512), BF16),
            pltpu.VMEM((27, 16, 8, 128), F32),
            pltpu.VMEM((3, 27, 4, 8, 128), F32),
            pltpu.VMEM((3, 27, 8, 128), F32),
            pltpu.VMEM((2 * len(PAIRS), 7, 8, 128), F32),
            pltpu.VMEM((7, sum(ALONG_Z) + 1, 2, 8, 128), F32),
            pltpu.VMEM((len(ALONG_Z) + 1, 15, 8, 128), F32),
            pltpu.SemaphoreType.DMA((SEMAPHORES[0],)),
            pltpu.SemaphoreType.DMA((SEMAPHORES[1],)),
            pltpu.SemaphoreType.DMA((4,)),
        ],
        compiler_params=pltpu.CompilerParams(
            collective_id=0, has_side_effects=True, vmem_limit_bytes=32 * 1024 * 1024
        ),
        cost_estimate=pl.CostEstimate(flops=6 * 4 * 226492416, bytes_accessed=8 * 1024 * 1024, transcendentals=32768),
    )(*(pltpu.with_memory_space_constraint(a, pltpu.HBM) for a in (clip, cotangent, kernel_one.reshape(27, 128, 128), kernel_two.reshape(27, 128, 128))))
    grad = jax.ShapeDtypeStruct((27, 16, 8, 128), F32)
    block_out, grad_clip, grad_one, grad_two = pl.pallas_call(
        copy_out,
        out_shape=(field, field, grad, grad),
        in_specs=[anywhere] * 3,
        out_specs=(hbm,) * 4,
        scratch_shapes=[pltpu.SemaphoreType.DMA((8,))],
        compiler_params=pltpu.CompilerParams(vmem_limit_bytes=1024 * 1024),
        cost_estimate=pl.CostEstimate(flops=0, bytes_accessed=8 * 1024 * 1024, transcendentals=0),
    )(block_out, grad_clip, sums)
    return block_out, grad_clip, grad_one.reshape(kernel_one.shape), grad_two.reshape(kernel_two.shape)


def solution(mesh):
    field = P("tm", "rows", None, None)
    return jax.shard_map(
        per_device,
        mesh=mesh,
        in_specs=(field, P(), P(), field),
        out_specs=(field, field, P(), P()),
        check_vma=False,
    )
```
